512 devices in a mesh: blk: 64 (over y_lo, z, core), uly: 8 (over x, y_hi).
Axes of the slice: x: 4, y: 8 (y_hi: 2, y_lo: 4; y = y_hi * 4 + y_lo), z: 8, core: 2. Of those that a mesh axis runs over, the one named last changes fastest.
Arguments:
- queries: bfloat16 [36864, 3072], P(('blk', 'uly')), may hold values from -17.5 to 17.5
- keys: bfloat16 [36864, 3072], P(('blk', 'uly')), may hold values from -10.2 to 10.2
- values: bfloat16 [36864, 3072], P(('blk', 'uly')), may hold values from -6 to 6
- tile_pairs: int32 [192, 8], replicated, may hold values from 0 to 191, as said below
- tile_coords: int32 [192, 3], replicated, may hold values from 0 to 31, as said below
Outputs:
- attended: bfloat16 [36864, 3072], P(('blk', 'uly'))
The draws below stay inside these ranges and needn't reach their ends.
Inputs may be any that keep to these rules, and one draw needn't show every extreme that they name: Tile index t stands for the grid cell (t % 2, (t // 2) % 3, t // 6); tile_pairs[t] lists the 8 distinct tiles of a block of 2 frames x 2 rows x 2 columns of cells that holds tile t's cell; every listed tile lies within 9 positions of t in the tile order, and that distance is reached. tile_coords gives every cell of the 2 x 3 x 32 tile grid once: tile t's cell as in tile_pairs, each of the three coordinates possibly mirrored over the whole grid.
All inputs are finite; a program needn't handle non-finite values.
Results may differ from the reference program's by a relative error of at most 0.009.
Values may be sent and summed in bfloat16 or wider, within the bound.
A program may use at most 64 MiB of HBM per device.

```python
import math
import jax
import jax.numpy as jnp
from jax import lax

HEADS = 24
HEAD_DIM = 128
TF = 3
TH = 8
TW = 8
GF = 2
GH = 3
KPT = 8
TILE = 192
TILES = 192
GW = 32
TOKENS = 36864


def grid_parts():
    tile_index = jnp.arange(TILES, dtype=jnp.int32)
    return (tile_index % GF, tile_index // GF % GH, tile_index // (GF * GH))


def draw_queries(key, part):
    own_key = jax.random.fold_in(key, 3)
    full_shape = (TOKENS, HEADS * HEAD_DIM)
    drawn = 1.7 * jax.random.truncated_normal(own_key, -6.0, 6.0, full_shape, jnp.float32)
    return drawn.astype(jnp.bfloat16)


def draw_keys(key, part):
    own_key = jax.random.fold_in(key, 4)
    full_shape = (TOKENS, HEADS * HEAD_DIM)
    drawn = 1.7 * jax.random.truncated_normal(own_key, -6.0, 6.0, full_shape, jnp.float32)
    return drawn.astype(jnp.bfloat16)


def draw_tile_pairs(key, part):
    key = jax.random.fold_in(key, 5)
    frame_index, height, across = grid_parts()
    choose = jax.random.randint(key, (TILES, 3), 0, 2, dtype=jnp.int32)
    lowest_frame = jnp.clip(frame_index - choose[:, 0], 0, GF - 2)
    lowest_row = jnp.clip(height - choose[:, 1], 0, GH - 2)
    lowest_col = jnp.clip(across - choose[:, 2], 0, GW - 2)
    slot_index = jnp.arange(KPT, dtype=jnp.int32)
    frame_step = slot_index // 4
    row_step = slot_index // 2 % 2
    col_step = slot_index % 2
    listed = lowest_frame[:, None] + frame_step[None, :] + GF * (lowest_row[:, None] + row_step[None, :])
    listed = listed + GF * GH * (lowest_col[:, None] + col_step[None, :])
    return listed.astype(jnp.int32)


def draw_tile_coords(key, part):
    key = jax.random.fold_in(key, 7)
    frame_index, height, across = grid_parts()
    flip_bits = jax.random.randint(key, (3,), 0, 2, dtype=jnp.int32)
    frame_coord = jnp.where(flip_bits[0] == 1, GF - 1 - frame_index, frame_index)
    height_coord = jnp.where(flip_bits[1] == 1, GH - 1 - height, height)
    width_coord = jnp.where(flip_bits[2] == 1, GW - 1 - across, across)
    return jnp.stack((frame_coord, height_coord, width_coord), axis=1).astype(jnp.int32)


def steps_of(stream_key, extent, cuts, low, high):
    gain = 1.0
    for dim, blocks in cuts:
        steps = jax.random.uniform(jax.random.fold_in(jax.random.fold_in(stream_key, 6), dim), (blocks,), jnp.float32, low / len(cuts), high / len(cuts))
        gain = gain * jnp.repeat(jnp.exp(steps), extent[dim] // blocks).reshape((-1,) + (1,) * (len(extent) - 1 - dim))
    return gain


def gaussian(key, shape, spread, reach, pieces=(), held_as=jnp.bfloat16):
    values = spread * jax.random.normal(key, shape, jnp.float32)
    if pieces:
        values = values * steps_of(key, shape, pieces, -0.22, 0.18)
    return jnp.clip(values, -reach, reach).astype(held_as)


def setup_inputs(seed: int = 0) -> dict:
    key_of = jax.random.split(jax.random.key(seed), 6)
    return {
        "queries": draw_queries(jax.random.fold_in(key_of[5], 71), 0),
        "keys": draw_keys(jax.random.fold_in(key_of[5], 71), 0),
        "values": gaussian(key_of[2], (TOKENS, HEADS * HEAD_DIM), 1.0, 6.0, ((0, 512),)),
        "tile_pairs": draw_tile_pairs(jax.random.fold_in(key_of[5], 71), 0),
        "tile_coords": draw_tile_coords(jax.random.fold_in(key_of[5], 71), 0),
    }


def rope_angles(coords):
    offset = jnp.arange(TILE, dtype=jnp.int32)
    frame_pos = (coords[:, 0:1] * TF + offset[None, :] // (TH * TW)).astype(jnp.float32)
    height_pos = (coords[:, 1:2] * TH + (offset[None, :] // TW) % TH).astype(jnp.float32)
    width_pos = (coords[:, 2:3] * TW + offset[None, :] % TW).astype(jnp.float32)
    halves = HEAD_DIM // 2
    side_pairs = HEAD_DIM // 6
    frame_pairs = halves - 2 * side_pairs
    pair_index = jnp.arange(halves, dtype=jnp.int32)
    within = jnp.where(pair_index < frame_pairs, pair_index,
                       jnp.where(pair_index < frame_pairs + side_pairs, pair_index - frame_pairs,
                                 pair_index - frame_pairs - side_pairs)).astype(jnp.float32)
    axis_len = jnp.where(pair_index < frame_pairs, frame_pairs, side_pairs).astype(jnp.float32)
    frequency = jnp.exp(-math.log(10000.0) * within / axis_len)
    angles = jnp.where(pair_index < frame_pairs, frame_pos[..., None] * frequency,
                       jnp.where(pair_index < frame_pairs + side_pairs, height_pos[..., None] * frequency,
                                 width_pos[..., None] * frequency))
    return jnp.cos(angles), jnp.sin(angles)


def rotate(tensor, cosine_table, sine_table):
    halves = HEAD_DIM // 2
    first_half = tensor[..., :halves].astype(jnp.float32)
    second_half = tensor[..., halves:].astype(jnp.float32)
    cosine_part = cosine_table[:, :, None, :]
    sine_part = sine_table[:, :, None, :]
    joined = jnp.concatenate((first_half * cosine_part - second_half * sine_part,
                              first_half * sine_part + second_half * cosine_part), axis=-1)
    return joined.astype(jnp.bfloat16)


def attend(query_tile, key_rows, value_rows):
    scaling = HEAD_DIM ** -0.5
    scores = jnp.einsum('qhd,khd->hqk', query_tile.astype(jnp.float32), key_rows.astype(jnp.float32)) * scaling
    row_max = jnp.max(scores, axis=2, keepdims=True)
    weights = jnp.exp(scores - row_max)
    row_total = jnp.sum(weights, axis=2, keepdims=True)
    rounded = weights.astype(jnp.bfloat16)
    summed = jnp.einsum('hqk,khd->qhd', rounded.astype(jnp.float32), value_rows.astype(jnp.float32))
    return (summed / jnp.transpose(row_total, (1, 0, 2))).astype(jnp.bfloat16)


def reference(queries, keys, values, tile_pairs, tile_coords):
    cosine_table, sine_table = rope_angles(tile_coords)
    grid_shape = (TILES, TILE, HEADS, HEAD_DIM)
    rotated_q = rotate(queries.reshape(grid_shape), cosine_table, sine_table)
    rotated_k = rotate(keys.reshape(grid_shape), cosine_table, sine_table)
    value_grid = values.reshape(grid_shape)

    def one_tile(inputs):
        query_tile, listed = inputs
        key_block = jnp.take(rotated_k, listed, axis=0).reshape(KPT * TILE, HEADS, HEAD_DIM)
        value_block = jnp.take(value_grid, listed, axis=0).reshape(KPT * TILE, HEADS, HEAD_DIM)
        return attend(query_tile, key_block, value_block)

    attended = lax.map(one_tile, (rotated_q, tile_pairs))
    return attended.reshape(TOKENS, HEADS * HEAD_DIM)
```

```python
import functools
import math

import jax
import jax.numpy as jnp
from jax import lax
from jax.experimental import pallas as pl
from jax.experimental.pallas import tpu as pltpu
from jax.sharding import PartitionSpec as P

HEAD_DIM = 128
TF = 3
TH = 8
TW = 8
GF = 2
GH = 3
KPT = 8
TILE = 192
MESH = pl.DeviceIdType.MESH


def rope_tables(tile_coords, first_token, count):
    token = first_token + jnp.arange(count, dtype=jnp.int32)
    offset = token % TILE
    first_tile = first_token // TILE
    near = lax.dynamic_slice_in_dim(tile_coords, first_tile, 1, 0)
    far = lax.dynamic_slice_in_dim(tile_coords, (first_token + count - 1) // TILE, 1, 0)
    coords = jnp.where((token // TILE == first_tile)[:, None], near, far)
    frame_pos = (coords[:, 0] * TF + offset // (TH * TW)).astype(jnp.float32)
    height_pos = (coords[:, 1] * TH + offset // TW % TH).astype(jnp.float32)
    width_pos = (coords[:, 2] * TW + offset % TW).astype(jnp.float32)
    halves = HEAD_DIM // 2
    side_pairs = HEAD_DIM // 6
    frame_pairs = halves - 2 * side_pairs
    lane = jnp.arange(HEAD_DIM, dtype=jnp.int32)
    pair = lane % halves
    in_frame = pair < frame_pairs
    in_height = pair < frame_pairs + side_pairs
    within = jnp.where(
        in_frame, pair, jnp.where(in_height, pair - frame_pairs, pair - frame_pairs - side_pairs)
    ).astype(jnp.float32)
    axis_len = jnp.where(in_frame, frame_pairs, side_pairs).astype(jnp.float32)
    frequency = jnp.exp(-math.log(10000.0) * within / axis_len)
    position = jnp.where(
        in_frame, frame_pos[:, None], jnp.where(in_height, height_pos[:, None], width_pos[:, None])
    )
    angles = position * frequency
    sign = jnp.where(lane < halves, -1.0, 1.0)
    return jnp.cos(angles), jnp.sin(angles) * sign


def kernel(
    uly, heads_here, cols,
    sel_ref, cos_ref, sin_ref, q_ref, k_ref, v_ref,
    out_ref,
    kv_stage, q_stage, kv_in, q_in, win0, win1, win2, q_rows, o_rows, o_stage,
    kv_ssem, kv_rsem, q_ssem, q_rsem, z_ssem, z_rsem, f_ssem, f_rsem, o_ssem, o_rsem,
):
    wins = (win0, win1, win2)
    heads = uly * heads_here
    chunk = q_ref.shape[0]
    run = chunk * uly
    blk = lax.axis_index("blk")
    me = lax.axis_index("uly")
    core = lax.rem(blk, 2)
    col = lax.div(blk, 2)
    has_left = col > 0
    has_right = col < cols - 1
    peers = [lax.rem(me + step, uly) for step in (1, 3, 5, 7, 2, 6, 4)]
    other = blk + 1 - 2 * core

    barrier = pltpu.get_barrier_semaphore()
    for peer in peers:
        pl.semaphore_signal(barrier, inc=1, device_id=(blk, peer), device_id_type=MESH)
    pl.semaphore_signal(barrier, inc=1, device_id=(other, me), device_id_type=MESH)

    @pl.when(has_left)
    def _():
        pl.semaphore_signal(barrier, inc=1, device_id=(blk - 2, me), device_id_type=MESH)

    @pl.when(has_right)
    def _():
        pl.semaphore_signal(barrier, inc=1, device_id=(blk + 2, me), device_id_type=MESH)

    cosine = cos_ref[...]
    sine = sin_ref[...]

    def rotated(rows):
        rows = rows.astype(jnp.float32)
        return (rows * cosine + pltpu.roll(rows, HEAD_DIM // 2, 1) * sine).astype(jnp.bfloat16)

    def stage_kv(head, carry):
        lanes = pl.ds(pl.multiple_of(head * HEAD_DIM, HEAD_DIM), HEAD_DIM)
        kv_stage[head, 0] = rotated(k_ref[:, lanes])
        kv_stage[head, 1] = v_ref[:, lanes]
        return carry

    def stage_q(head, carry):
        lanes = pl.ds(pl.multiple_of(head * HEAD_DIM, HEAD_DIM), HEAD_DIM)
        q_stage[head] = rotated(q_ref[:, lanes])
        return carry

    lax.fori_loop(0, heads, stage_kv, 0)
    pl.semaphore_wait(barrier, uly + has_left.astype(jnp.int32) + has_right.astype(jnp.int32))

    def exchange(stage, landing, ssem, rsem, j):
        for peer in peers:
            pltpu.make_async_remote_copy(
                src_ref=stage.at[peer * heads_here + j],
                dst_ref=landing.at[j, me],
                send_sem=ssem.at[j],
                recv_sem=rsem.at[j],
                device_id=(blk, peer),
                device_id_type=MESH,
            ).start()
        pltpu.make_async_copy(
            stage.at[me * heads_here + j], landing.at[j, me], rsem.at[j]
        ).start()

    for j in range(heads_here):
        exchange(kv_stage, kv_in, kv_ssem, kv_rsem, j)
    lax.fori_loop(0, heads, stage_q, 0)
    for j in range(heads_here):
        exchange(q_stage, q_in, q_ssem, q_rsem, j)

    tiles = run // TILE
    mine = pl.ds(core * tiles, tiles)
    theirs = pl.ds((1 - core) * tiles, tiles)

    def to_other(j, slot):
        rows = wins[j].at[slot, mine]
        return pltpu.make_async_remote_copy(
            src_ref=rows, dst_ref=rows, send_sem=f_ssem.at[j, slot], recv_sem=f_rsem.at[j, slot],
            device_id=(other, me), device_id_type=MESH,
        )

    def from_other(j, slot):
        rows = wins[j].at[slot, theirs]
        return pltpu.make_async_copy(rows, rows, f_rsem.at[j, slot])

    def to_left(j):
        return pltpu.make_async_remote_copy(
            src_ref=wins[j].at[1, mine], dst_ref=wins[j].at[2, mine],
            send_sem=z_ssem.at[j, 0], recv_sem=z_rsem.at[j, 0],
            device_id=(blk - 2, me), device_id_type=MESH,
        )

    def to_right(j):
        return pltpu.make_async_remote_copy(
            src_ref=wins[j].at[1, mine], dst_ref=wins[j].at[0, mine],
            send_sem=z_ssem.at[j, 1], recv_sem=z_rsem.at[j, 1],
            device_id=(blk + 2, me), device_id_type=MESH,
        )

    def gather_rows(landing, index, store):
        for pair in range(uly // 2):
            both = jnp.concatenate(
                [landing[index(2 * pair)].astype(jnp.float32), landing[index(2 * pair + 1)].astype(jnp.float32)],
                axis=0,
            ).astype(jnp.bfloat16)
            first, past = 2 * chunk * pair, 2 * chunk * (pair + 1)
            for tile in range(first // TILE, (past - 1) // TILE + 1):
                start, stop = max(first, tile * TILE), min(past, (tile + 1) * TILE)
                store(tile, start - tile * TILE, both[start - first : stop - first])

    def spread(j):
        pltpu.make_async_copy(kv_in.at[j], kv_in.at[j], kv_rsem.at[j]).wait()
        for which in range(2):
            def store(tile, row, value):
                wins[j][1, core * tiles + tile, which, pl.ds(row, value.shape[0])] = value
            gather_rows(kv_in, lambda s: (j, s, which), store)

        @pl.when(has_right)
        def _():
            to_right(j).start()

        @pl.when(has_left)
        def _():
            to_left(j).start()

        to_other(j, 1).start()

    def forward(j):
        @pl.when(has_left)
        def _():
            rows = wins[j].at[0, mine]
            pltpu.make_async_copy(rows, rows, z_rsem.at[j, 1]).wait()
            to_other(j, 0).start()

        @pl.when(has_right)
        def _():
            rows = wins[j].at[2, mine]
            pltpu.make_async_copy(rows, rows, z_rsem.at[j, 0]).wait()
            to_other(j, 2).start()

    factor = HEAD_DIM ** -0.5 * math.log2(math.e)
    listed = KPT // 2

    def attend(j):
        pltpu.make_async_copy(q_in.at[j], q_in.at[j], q_rsem.at[j]).wait()
        def store(tile, row, value):
            q_rows[tile, pl.ds(row, value.shape[0])] = value
        gather_rows(q_in, lambda s: (j, s), store)
        from_other(j, 1).wait()

        @pl.when(has_left)
        def _():
            from_other(j, 0).wait()

        @pl.when(has_right)
        def _():
            from_other(j, 2).wait()

        def one_tile(tile, carry):
            side = sel_ref[tile, 0]
            first = sel_ref[tile, 1]

            def rows_of(slot, which):
                return jnp.concatenate(
                    [wins[j][slot, first + step, which] for step in range(listed)], axis=0
                )

            rows = pl.ds(pl.multiple_of(tile * TILE, TILE), TILE)
            query = q_rows[tile]
            contract = (((1,), (1,)), ((), ()))
            near = lax.dot_general(
                query, rows_of(1, 0), contract, preferred_element_type=jnp.float32
            )
            far = lax.dot_general(
                query, rows_of(side, 0), contract, preferred_element_type=jnp.float32
            )
            largest = jnp.maximum(
                jnp.max(near, axis=1, keepdims=True), jnp.max(far, axis=1, keepdims=True)
            )
            near = jnp.exp2((near - largest) * factor)
            far = jnp.exp2((far - largest) * factor)
            total = jnp.sum(near, axis=1, keepdims=True) + jnp.sum(far, axis=1, keepdims=True)
            summed = jnp.dot(
                near.astype(jnp.bfloat16), rows_of(1, 1), preferred_element_type=jnp.float32
            ) + jnp.dot(
                far.astype(jnp.bfloat16), rows_of(side, 1), preferred_element_type=jnp.float32
            )
            o_rows[rows] = summed / total
            return carry

        lax.fori_loop(0, tiles, one_tile, 0)
        for part in range(uly):
            o_stage[j, part] = o_rows[pl.ds(part * chunk, chunk)].astype(jnp.bfloat16)
        lanes = pl.ds(pl.multiple_of((me * heads_here + j) * HEAD_DIM, HEAD_DIM), HEAD_DIM)
        for peer in peers:
            pltpu.make_async_remote_copy(
                src_ref=o_stage.at[j, peer],
                dst_ref=out_ref.at[:, lanes],
                send_sem=o_ssem.at[j],
                recv_sem=o_rsem,
                device_id=(blk, peer),
                device_id_type=MESH,
            ).start()
        pltpu.make_async_copy(o_stage.at[j, me], out_ref.at[:, lanes], o_rsem).start()

    spread(0)
    spread(1)
    forward(0)
    spread(2)
    forward(1)
    attend(0)
    forward(2)
    attend(1)
    attend(2)

    sent = pl.ds(0, uly - 1)
    for j in range(heads_here):
        pltpu.make_async_copy(kv_in.at[j, sent], kv_in.at[j, sent], kv_ssem.at[j]).wait()
        pltpu.make_async_copy(q_in.at[j, sent], q_in.at[j, sent], q_ssem.at[j]).wait()
        to_other(j, 1).wait_send()

        @pl.when(has_left)
        def _():
            to_left(j).wait_send()
            to_other(j, 0).wait_send()

        @pl.when(has_right)
        def _():
            to_right(j).wait_send()
            to_other(j, 2).wait_send()

        pltpu.make_async_copy(o_stage.at[j, sent], o_stage.at[j, sent], o_ssem.at[j]).wait()
    pltpu.make_async_copy(out_ref, out_ref, o_rsem).wait()


def on_device(cols, queries, keys, values, tile_pairs, tile_coords):
    uly = lax.axis_size("uly")
    chunk, columns = queries.shape
    heads_here = columns // HEAD_DIM // uly
    run = chunk * uly
    tiles = run // TILE
    blk = lax.axis_index("blk")
    first_token = blk * run + lax.axis_index("uly") * chunk
    cosine, sine = rope_tables(tile_coords, first_token, chunk)
    lowest = jnp.min(lax.dynamic_slice_in_dim(tile_pairs, blk * tiles, tiles, 0), axis=1)
    side = 2 * (lowest // (GF * GH) - blk // 2 + 1)
    first = lowest % (GF * GH)
    sel = jnp.stack((side, first), axis=1)
    vmem = pl.BlockSpec(memory_space=pltpu.VMEM)
    dma = pltpu.SemaphoreType.DMA
    bf16 = jnp.bfloat16
    heads = uly * heads_here
    window = pltpu.VMEM((3, 2 * tiles, 2, TILE, HEAD_DIM), bf16)
    return pl.pallas_call(
        functools.partial(kernel, uly, heads_here, cols),
        out_shape=jax.ShapeDtypeStruct(queries.shape, bf16),
        in_specs=[pl.BlockSpec(memory_space=pltpu.SMEM)] + [vmem] * 5,
        out_specs=vmem,
        scratch_shapes=[
            pltpu.VMEM((heads, 2, chunk, HEAD_DIM), bf16),
            pltpu.VMEM((heads, chunk, HEAD_DIM), bf16),
            pltpu.VMEM((heads_here, uly, 2, chunk, HEAD_DIM), bf16),
            pltpu.VMEM((heads_here, uly, chunk, HEAD_DIM), bf16),
            window, window, window,
            pltpu.VMEM((tiles, TILE, HEAD_DIM), bf16),
            pltpu.VMEM((run, HEAD_DIM), jnp.float32),
            pltpu.VMEM((heads_here, uly, chunk, HEAD_DIM), bf16),
            dma((heads_here,)), dma((heads_here,)),
            dma((heads_here,)), dma((heads_here,)),
            dma((heads_here, 2)), dma((heads_here, 2)),
            dma((heads_here, 3)), dma((heads_here, 3)),
            dma((heads_here,)), dma(()),
        ],
        compiler_params=pltpu.CompilerParams(
            collective_id=0, has_side_effects=True, vmem_limit_bytes=40 * 2 ** 20
        ),
    )(sel, cosine, sine, queries, keys, values)


def solution(mesh):
    spec = P(("blk", "uly"), None)
    return jax.shard_map(
        functools.partial(on_device, mesh.shape["blk"] // 2),
        mesh=mesh,
        in_specs=(spec, spec, spec, P(), P()),
        out_specs=spec,
        check_vma=False,
    )
```

```python
import functools
import math

import jax
import jax.numpy as jnp
from jax import lax
from jax.experimental import pallas as pl
from jax.experimental.pallas import tpu as pltpu
from jax.sharding import PartitionSpec as P

HEAD_DIM = 128
TF = 3
TH = 8
TW = 8
GF = 2
GH = 3
KPT = 8
TILE = 192
LINE = 8
MESH = pl.DeviceIdType.MESH


def rope_tables(coords, row, offset, count):
    shape = (count, HEAD_DIM)
    token = lax.broadcasted_iota(jnp.int32, shape, 0) + offset
    lane = lax.broadcasted_iota(jnp.int32, shape, 1)
    past = token >= TILE
    token = jnp.where(past, token - TILE, token)
    last = row + lax.div(offset + count - 1, TILE)

    def cell(axis):
        return jnp.where(past, coords[last, axis], coords[row, axis])

    halves = HEAD_DIM // 2
    side_pairs = HEAD_DIM // 6
    frame_pairs = halves - 2 * side_pairs
    pair = jnp.where(lane < halves, lane, lane - halves)
    in_frame = pair < frame_pairs
    in_height = pair < frame_pairs + side_pairs
    within = jnp.where(
        in_frame, pair, jnp.where(in_height, pair - frame_pairs, pair - frame_pairs - side_pairs)
    ).astype(jnp.float32)
    axis_len = jnp.where(in_frame, float(frame_pairs), float(side_pairs))
    frequency = jnp.exp(-math.log(10000.0) * within / axis_len)
    position = jnp.where(
        in_frame,
        cell(0) * TF + lax.div(token, TH * TW),
        jnp.where(
            in_height,
            cell(1) * TH + lax.rem(lax.div(token, TW), TH),
            cell(2) * TW + lax.rem(token, TW),
        ),
    ).astype(jnp.float32)
    angles = position * frequency
    return jnp.cos(angles), jnp.where(lane < halves, -jnp.sin(angles), jnp.sin(angles))


def kernel(
    uly, heads_here, cols, line,
    q_hbm, k_hbm, v_hbm, pairs_hbm, coords_hbm,
    out_ref,
    kv_stage, q_stage, kv_in, q_in, win0, win1, win2, q_rows, o_rows, o_stage,
    kv_ssem, kv_rsem, q_ssem, q_rsem, z_ssem, z_rsem, f_ssem, f_rsem, o_ssem, o_rsem,
    relay_buf, r_ssem, r_rsem, q_ref, k_ref, v_ref, pairs, coords, in_sem,
):
    wins = (win0, win1, win2)
    heads = uly * heads_here
    chunk = q_ref.shape[0]
    run = chunk * uly
    blk = lax.axis_index("blk")
    me = lax.axis_index("uly")
    tiles = run // TILE
    some = pairs.shape[0]
    window_row = jnp.minimum(lax.div(blk * tiles, 8) * 8, pairs_hbm.shape[0] - some)
    near_rows = pl.ds(pl.multiple_of(window_row, 8), some)
    loads = [
        pltpu.make_async_copy(src, dst, in_sem.at[n])
        for n, (src, dst) in enumerate((
            (coords_hbm.at[near_rows], coords),
            (k_hbm, k_ref),
            (v_hbm, v_ref),
            (q_hbm, q_ref),
            (pairs_hbm.at[near_rows], pairs),
        ))
    ]
    for load in loads:
        load.start()
    core = lax.rem(blk, 2)
    col = lax.div(blk, 2)
    has_left = col > 0
    has_right = col < cols - 1
    place = lax.rem(col, line)
    cross_left = (place == 0) & has_left
    cross_right = (place == line - 1) & has_right
    bend_right = (place == 0) & (col < cols - line)
    bend_left = (place == line - 1) & (col >= line)
    skip_right = (place == line - 2) & (col < cols - line)
    skip_left = (place == 1) & (col >= line)
    row = 2 * line
    peers = [lax.rem(me + step, uly) for step in (1, 3, 5, 7, 2, 6, 4)]
    other = blk + 1 - 2 * core

    barrier = pltpu.get_barrier_semaphore()
    for peer in peers:
        pl.semaphore_signal(barrier, inc=1, device_id=(blk, peer), device_id_type=MESH)
    pl.semaphore_signal(barrier, inc=1, device_id=(other, me), device_id_type=MESH)

    @pl.when(has_left)
    def _():
        pl.semaphore_signal(barrier, inc=1, device_id=(blk - 2, me), device_id_type=MESH)

    @pl.when(has_right)
    def _():
        pl.semaphore_signal(barrier, inc=1, device_id=(blk + 2, me), device_id_type=MESH)

    extra = (
        (cross_left, blk - row),
        (cross_left, blk + row - 2),
        (cross_left, blk - 4),
        (cross_right, blk + row),
        (cross_right, blk - row + 2),
        (cross_right, blk + 4),
        (bend_right, blk + row - 2),
        (bend_right, blk + row),
        (bend_left, blk - row + 2),
        (bend_left, blk - row),
        (skip_right, blk + 4),
        (skip_left, blk - 4),
    )
    greeted = uly
    for due, target in ((has_left, None), (has_right, None)) + extra:
        greeted = greeted + due.astype(jnp.int32)
    for due, target in extra:

        @pl.when(due)
        def _():
            pl.semaphore_signal(barrier, inc=1, device_id=(target, me), device_id_type=MESH)

    loads[0].wait()
    cosine, sine = rope_tables(
        coords,
        blk * tiles + lax.div(me * chunk, TILE) - window_row,
        lax.rem(me * chunk, TILE),
        chunk,
    )

    def rotated(rows):
        rows = rows.astype(jnp.float32)
        return (rows * cosine + pltpu.roll(rows, HEAD_DIM // 2, 1) * sine).astype(jnp.bfloat16)

    def stage_kv(j, peer, carry):
        head = peer * heads_here + j
        lanes = pl.ds(pl.multiple_of(head * HEAD_DIM, HEAD_DIM), HEAD_DIM)
        kv_stage[head, 0] = rotated(k_ref[:, lanes])
        kv_stage[head, 1] = v_ref[:, lanes]
        return carry

    def stage_q(j, peer, carry):
        head = peer * heads_here + j
        lanes = pl.ds(pl.multiple_of(head * HEAD_DIM, HEAD_DIM), HEAD_DIM)
        q_stage[head] = rotated(q_ref[:, lanes])
        return carry

    loads[1].wait()
    loads[2].wait()
    lax.fori_loop(0, uly, functools.partial(stage_kv, 0), 0)
    pl.semaphore_wait(barrier, greeted)

    def exchange(stage, landing, ssem, rsem, j):
        for peer in peers:
            pltpu.make_async_remote_copy(
                src_ref=stage.at[peer * heads_here + j],
                dst_ref=landing.at[j, me],
                send_sem=ssem.at[j],
                recv_sem=rsem.at[j],
                device_id=(blk, peer),
                device_id_type=MESH,
            ).start()
        pltpu.make_async_copy(
            stage.at[me * heads_here + j], landing.at[j, me], rsem.at[j]
        ).start()

    for j in range(heads_here):
        if j:
            lax.fori_loop(0, uly, functools.partial(stage_kv, j), 0)
        exchange(kv_stage, kv_in, kv_ssem, kv_rsem, j)
    loads[3].wait()
    for j in range(heads_here):
        lax.fori_loop(0, uly, functools.partial(stage_q, j), 0)
    loads[4].wait()

    choice = []
    for tile in range(tiles):
        row_here = blk * tiles + tile - window_row
        lowest = pairs[row_here, 0]
        for slot in range(1, KPT):
            lowest = jnp.minimum(lowest, pairs[row_here, slot])
        across = lax.div(lowest, GF * GH)
        choice.append((
            jnp.where(across < col, 0, 2),
            jnp.clip(lowest - across * (GF * GH), 0, GF * GH - KPT // 2),
        ))

    mine = pl.ds(core * tiles, tiles)
    theirs = pl.ds((1 - core) * tiles, tiles)

    def to_other(j, slot):
        rows = wins[j].at[slot, mine]
        return pltpu.make_async_remote_copy(
            src_ref=rows, dst_ref=rows, send_sem=f_ssem.at[j, slot], recv_sem=f_rsem.at[j, slot],
            device_id=(other, me), device_id_type=MESH,
        )

    def from_other(j, slot):
        rows = wins[j].at[slot, theirs]
        return pltpu.make_async_copy(rows, rows, f_rsem.at[j, slot])

    def hop(src, dst, ssem, rsem, target):
        return pltpu.make_async_remote_copy(
            src_ref=src, dst_ref=dst, send_sem=ssem, recv_sem=rsem,
            device_id=(target, me), device_id_type=MESH,
        )

    last = tiles - 1

    def part(n):
        return core * tiles + last if n == 0 else pl.ds(core * tiles, last)

    def to_side(j, slot, target, n):
        return hop(
            wins[j].at[1, part(n)], wins[j].at[2 - slot, part(n)],
            z_ssem.at[j, slot // 2, n], z_rsem.at[j, 1 - slot // 2, n], target,
        )

    def direct(j, slot, target):
        return hop(
            wins[j].at[1, core * tiles], wins[j].at[2 - slot, core * tiles],
            z_ssem.at[j, slot // 2, 0], z_rsem.at[j, 1 - slot // 2, 0], target,
        )

    def bend_in(j, target):
        return hop(
            wins[j].at[1, core * tiles + 1], relay_buf.at[j],
            r_ssem.at[j, 0], r_rsem.at[j], target,
        )

    def bend_out(j, slot, target):
        return hop(
            relay_buf.at[j], wins[j].at[slot, core * tiles + 1],
            r_ssem.at[j, 1], z_rsem.at[j, slot // 2, 1], target,
        )

    def skip_out(j, slot, target):
        return hop(
            wins[j].at[slot, core * tiles + last], wins[j].at[2 - slot, core * tiles + last],
            r_ssem.at[j, 1], z_rsem.at[j, 1 - slot // 2, 2], target,
        )

    inner_right = has_right & ~cross_right
    inner_left = has_left & ~cross_left

    def sides(j):
        return (
            (cross_right, bend_in(j, blk - row + 2)),
            (cross_left, bend_in(j, blk + row - 2)),
            (inner_right, to_side(j, 2, blk + 2, 0)),
            (inner_left, to_side(j, 0, blk - 2, 0)),
            (cross_right, direct(j, 2, blk + 2)),
            (cross_left, direct(j, 0, blk - 2)),
            (inner_right, to_side(j, 2, blk + 2, 1)),
            (inner_left, to_side(j, 0, blk - 2, 1)),
        )

    def relays(j):
        return (
            (bend_right, bend_out(j, 0, blk + row)),
            (bend_left, bend_out(j, 2, blk - row)),
            (skip_right, skip_out(j, 2, blk + 4)),
            (skip_left, skip_out(j, 0, blk - 4)),
        )

    def start_all(copies):
        for due, copy in copies:

            @pl.when(due)
            def _():
                copy.start()

    def sent_all(copies):
        for due, copy in copies:

            @pl.when(due)
            def _():
                copy.wait_send()

    def arrived(rows, sem):
        pltpu.make_async_copy(rows, rows, sem).wait()

    def gather_rows(landing, index, store):
        for pair in range(uly // 2):
            both = jnp.concatenate(
                [landing[index(2 * pair)].astype(jnp.float32), landing[index(2 * pair + 1)].astype(jnp.float32)],
                axis=0,
            ).astype(jnp.bfloat16)
            first, past = 2 * chunk * pair, 2 * chunk * (pair + 1)
            for tile in range(first // TILE, (past - 1) // TILE + 1):
                start, stop = max(first, tile * TILE), min(past, (tile + 1) * TILE)
                store(tile, start - tile * TILE, both[start - first : stop - first])

    def spread(j):
        pltpu.make_async_copy(kv_in.at[j], kv_in.at[j], kv_rsem.at[j]).wait()
        for which in range(2):
            def store(tile, row, value):
                wins[j][1, core * tiles + tile, which, pl.ds(row, value.shape[0])] = value
            gather_rows(kv_in, lambda s: (j, s, which), store)

        start_all(sides(j))
        to_other(j, 1).start()

    def relay(j):
        @pl.when(bend_left | bend_right)
        def _():
            arrived(relay_buf.at[j], r_rsem.at[j])

        for slot, due in ((0, skip_left), (2, skip_right)):

            @pl.when(due)
            def _():
                arrived(wins[j].at[slot, part(0)], z_rsem.at[j, slot // 2, 0])

        start_all(relays(j))

    def forward(j):
        for slot, inner, skips, cross in (
            (0, inner_left, skip_left, cross_left),
            (2, inner_right, skip_right, cross_right),
        ):

            @pl.when(inner)
            def _():
                @pl.when(~skips)
                def _():
                    arrived(wins[j].at[slot, part(0)], z_rsem.at[j, slot // 2, 0])

                arrived(wins[j].at[slot, part(1)], z_rsem.at[j, slot // 2, 1])
                to_other(j, slot).start()

            @pl.when(cross)
            def _():
                for n in range(tiles):
                    arrived(wins[j].at[slot, core * tiles + n], z_rsem.at[j, slot // 2, n])
                to_other(j, slot).start()

    factor = HEAD_DIM ** -0.5 * math.log2(math.e)
    listed = KPT // 2

    def attend(j):
        pltpu.make_async_copy(q_in.at[j], q_in.at[j], q_rsem.at[j]).wait()
        def store(tile, row, value):
            q_rows[tile, pl.ds(row, value.shape[0])] = value
        gather_rows(q_in, lambda s: (j, s), store)
        from_other(j, 1).wait()

        @pl.when(has_left)
        def _():
            from_other(j, 0).wait()

        @pl.when(has_right)
        def _():
            from_other(j, 2).wait()

        lanes = pl.ds(pl.multiple_of((me * heads_here + j) * HEAD_DIM, HEAD_DIM), HEAD_DIM)
        for tile in range(tiles):
            side, first = choice[tile]

            def rows_of(slot, which):
                return jnp.concatenate(
                    [wins[j][slot, first + step, which] for step in range(listed)], axis=0
                )

            query = q_rows[tile]
            contract = (((1,), (1,)), ((), ()))
            near = lax.dot_general(
                query, rows_of(1, 0), contract, preferred_element_type=jnp.float32
            )
            far = lax.dot_general(
                query, rows_of(side, 0), contract, preferred_element_type=jnp.float32
            )
            largest = jnp.maximum(
                jnp.max(near, axis=1, keepdims=True), jnp.max(far, axis=1, keepdims=True)
            )
            near = jnp.exp2((near - largest) * factor)
            far = jnp.exp2((far - largest) * factor)
            total = jnp.sum(near, axis=1, keepdims=True) + jnp.sum(far, axis=1, keepdims=True)
            summed = jnp.dot(
                near.astype(jnp.bfloat16), rows_of(1, 1), preferred_element_type=jnp.float32
            ) + jnp.dot(
                far.astype(jnp.bfloat16), rows_of(side, 1), preferred_element_type=jnp.float32
            )
            o_rows[pl.ds(tile * TILE, TILE)] = summed / total
            for part_ in range(tile * TILE // chunk, (tile + 1) * TILE // chunk):
                o_stage[j, part_] = o_rows[pl.ds(part_ * chunk, chunk)].astype(jnp.bfloat16)

                @pl.when(me == part_)
                def _():
                    pltpu.make_async_copy(
                        o_stage.at[j, part_], out_ref.at[:, lanes], o_rsem
                    ).start()

                @pl.when(me != part_)
                def _():
                    pltpu.make_async_remote_copy(
                        src_ref=o_stage.at[j, part_],
                        dst_ref=out_ref.at[:, lanes],
                        send_sem=o_ssem.at[j],
                        recv_sem=o_rsem,
                        device_id=(blk, part_),
                        device_id_type=MESH,
                    ).start()

    def queries(j):
        exchange(q_stage, q_in, q_ssem, q_rsem, j)

    spread(0)
    queries(0)
    relay(0)
    spread(1)
    queries(1)
    forward(0)
    relay(1)
    spread(2)
    queries(2)
    forward(1)
    attend(0)
    relay(2)
    attend(1)
    forward(2)
    attend(2)

    sent = pl.ds(0, uly - 1)
    for j in range(heads_here):
        pltpu.make_async_copy(kv_in.at[j, sent], kv_in.at[j, sent], kv_ssem.at[j]).wait()
        pltpu.make_async_copy(q_in.at[j, sent], q_in.at[j, sent], q_ssem.at[j]).wait()
        to_other(j, 1).wait_send()
        sent_all(sides(j) + relays(j))
        sent_all(((has_left, to_other(j, 0)), (has_right, to_other(j, 2))))
        pltpu.make_async_copy(o_stage.at[j, sent], o_stage.at[j, sent], o_ssem.at[j]).wait()
    pltpu.make_async_copy(out_ref, out_ref, o_rsem).wait()


def on_device(cols, line, queries, keys, values, tile_pairs, tile_coords):
    uly = lax.axis_size("uly")
    chunk, columns = queries.shape
    heads_here = columns // HEAD_DIM // uly
    run = chunk * uly
    tiles = run // TILE
    vmem = pl.BlockSpec(memory_space=pltpu.VMEM)
    dma = pltpu.SemaphoreType.DMA
    bf16 = jnp.bfloat16
    heads = uly * heads_here
    window = pltpu.VMEM((3, 2 * tiles, 2, TILE, HEAD_DIM), bf16)
    return pl.pallas_call(
        functools.partial(kernel, uly, heads_here, cols, line),
        out_shape=jax.ShapeDtypeStruct(queries.shape, bf16),
        in_specs=[pl.BlockSpec(memory_space=pl.ANY)] * 5,
        out_specs=vmem,
        scratch_shapes=[
            pltpu.VMEM((heads, 2, chunk, HEAD_DIM), bf16),
            pltpu.VMEM((heads, chunk, HEAD_DIM), bf16),
            pltpu.VMEM((heads_here, uly, 2, chunk, HEAD_DIM), bf16),
            pltpu.VMEM((heads_here, uly, chunk, HEAD_DIM), bf16),
            window, window, window,
            pltpu.VMEM((tiles, TILE, HEAD_DIM), bf16),
            pltpu.VMEM((run, HEAD_DIM), jnp.float32),
            pltpu.VMEM((heads_here, uly, chunk, HEAD_DIM), bf16),
            dma((heads_here,)), dma((heads_here,)),
            dma((heads_here,)), dma((heads_here,)),
            dma((heads_here, 2, 2)), dma((heads_here, 2, 3)),
            dma((heads_here, 3)), dma((heads_here, 3)),
            dma((heads_here,)), dma(()),
            pltpu.VMEM((heads_here, 2, TILE, HEAD_DIM), bf16), dma((heads_here, 2)), dma((heads_here,)),
            pltpu.VMEM(queries.shape, bf16), pltpu.VMEM(queries.shape, bf16), pltpu.VMEM(queries.shape, bf16),
            pltpu.SMEM((16, KPT), jnp.int32), pltpu.SMEM((16, 3), jnp.int32), dma((5,)),
        ],
        compiler_params=pltpu.CompilerParams(
            collective_id=0, has_side_effects=True, vmem_limit_bytes=56 * 2 ** 20
        ),
    )(queries, keys, values, tile_pairs, tile_coords)


def solution(mesh):
    spec = P(("blk", "uly"), None)
    return jax.shard_map(
        functools.partial(on_device, mesh.shape["blk"] // 2, LINE),
        mesh=mesh,
        in_specs=(spec, spec, spec, P(), P()),
        out_specs=spec,
        check_vma=False,
    )
```

```python
import functools
import math

import jax
import jax.numpy as jnp
from jax import lax
from jax.experimental import pallas as pl
from jax.experimental.pallas import tpu as pltpu
from jax.sharding import PartitionSpec as P

HEAD_DIM = 128
TF = 3
TH = 8
TW = 8
GF = 2
GH = 3
KPT = 8
TILE = 192
LINE = 8
MESH = pl.DeviceIdType.MESH
DIRECT = 0
SKIP = 4
BENDS = ((1, 0), (2, 1), (3, 2), (5, 5))


def rope_tables(coords, row, offset, count):
    shape = (count, HEAD_DIM)
    token = lax.broadcasted_iota(jnp.int32, shape, 0) + offset
    lane = lax.broadcasted_iota(jnp.int32, shape, 1)
    past = token >= TILE
    token = jnp.where(past, token - TILE, token)
    last = row + lax.div(offset + count - 1, TILE)

    def cell(axis):
        return jnp.where(past, coords[axis, last], coords[axis, row])

    halves = HEAD_DIM // 2
    side_pairs = HEAD_DIM // 6
    frame_pairs = halves - 2 * side_pairs
    pair = jnp.where(lane < halves, lane, lane - halves)
    in_frame = pair < frame_pairs
    in_height = pair < frame_pairs + side_pairs
    within = jnp.where(
        in_frame, pair, jnp.where(in_height, pair - frame_pairs, pair - frame_pairs - side_pairs)
    ).astype(jnp.float32)
    axis_len = jnp.where(in_frame, float(frame_pairs), float(side_pairs))
    frequency = jnp.exp(-math.log(10000.0) * within / axis_len)
    position = jnp.where(
        in_frame,
        cell(0) * TF + lax.div(token, TH * TW),
        jnp.where(
            in_height,
            cell(1) * TH + lax.rem(lax.div(token, TW), TH),
            cell(2) * TW + lax.rem(token, TW),
        ),
    ).astype(jnp.float32)
    angles = position * frequency
    return jnp.cos(angles), jnp.where(lane < halves, -jnp.sin(angles), jnp.sin(angles))


def kernel(
    uly, heads_here, cols, line,
    q_hbm, k_hbm, v_hbm, pairs_hbm, coords_hbm,
    out_ref,
    kv_stage, q_stage, kv_in, q_in, win0, win1, win2, q_rows, o_rows, o_stage,
    kv_ssem, kv_rsem, q_ssem, q_rsem, z_ssem, z_rsem, f_ssem, f_rsem, o_ssem, o_rsem,
    relay_buf, r_ssem, r_rsem, q_ref, k_ref, v_ref, pairs, coords, in_sem, go_sem,
):
    wins = (win0, win1, win2)
    heads = uly * heads_here
    chunk = q_ref.shape[0]
    run = chunk * uly
    blk = lax.axis_index("blk")
    me = lax.axis_index("uly")
    tiles = run // TILE
    loads = [
        pltpu.make_async_copy(src, dst, in_sem.at[n])
        for n, (src, dst) in enumerate((
            (coords_hbm, coords),
            (k_hbm, k_ref),
            (v_hbm, v_ref),
            (q_hbm, q_ref),
            (pairs_hbm, pairs),
        ))
    ]
    for load in loads:
        load.start()
    core = lax.rem(blk, 2)
    col = lax.div(blk, 2)
    has_left = col > 0
    has_right = col < cols - 1
    place = lax.rem(col, line)
    cross_left = (place == 0) & has_left
    cross_right = (place == line - 1) & has_right
    skip_right = (place == line - 2) & (col < cols - line)
    skip_left = (place == 1) & (col >= line)
    row = 2 * line
    span = row - 2
    bends = [
        (unit, (place == stop) & (col < cols - line), (place == line - 1 - stop) & (col >= line), 2 * stop)
        for unit, stop in BENDS
    ]
    peers = [lax.rem(me + step, uly) for step in (1, 3, 5, 7, 2, 6, 4)]
    other = blk + 1 - 2 * core

    barrier = pltpu.get_barrier_semaphore()
    for peer in peers:
        pl.semaphore_signal(barrier, inc=1, device_id=(blk - core, peer), device_id_type=MESH)
    pl.semaphore_signal(barrier, inc=1, device_id=(other, me), device_id_type=MESH)
    greeted = [
        (has_left, blk - 2),
        (has_right, blk + 2),
        (cross_left, blk - 4),
        (cross_right, blk + 4),
        (skip_right, blk + 4),
        (skip_left, blk - 4),
    ]
    for _, up, down, shift in bends:
        greeted += [
            (cross_left, blk + span - shift),
            (cross_left, blk - row + shift),
            (cross_right, blk - span + shift),
            (cross_right, blk + row - shift),
            (up, blk + span - shift),
            (up, blk + row - shift),
            (down, blk - span + shift),
            (down, blk - row + shift),
        ]
    columns_in = 0
    for due, target in greeted:
        columns_in = columns_in + due.astype(jnp.int32)

        @pl.when(due)
        def _():
            pl.semaphore_signal(
                barrier, inc=1, device_id=(target - core + 1, me), device_id_type=MESH
            )

    def tell_other():
        pl.semaphore_signal(go_sem, inc=1, device_id=(other, me), device_id_type=MESH)

    def wait_group():
        @pl.when(core == 0)
        def _():
            pl.semaphore_wait(barrier, 2 * (uly - 1) + 1)
            tell_other()

        @pl.when(core == 1)
        def _():
            pl.semaphore_wait(go_sem, 1)

    def wait_columns():
        @pl.when(core == 1)
        def _():
            pl.semaphore_wait(barrier, 2 * columns_in + 1)
            tell_other()

        @pl.when(core == 0)
        def _():
            pl.semaphore_wait(go_sem, 1)

    loads[0].wait()
    cosine, sine = rope_tables(
        coords,
        blk * tiles + lax.div(me * chunk, TILE),
        lax.rem(me * chunk, TILE),
        chunk,
    )

    def rotated(rows):
        rows = rows.astype(jnp.float32)
        return (rows * cosine + pltpu.roll(rows, HEAD_DIM // 2, 1) * sine).astype(jnp.bfloat16)

    def stage_kv(i, peer, carry):
        head = peer * heads_here + i // 2
        lanes = pl.ds(pl.multiple_of(head * HEAD_DIM, HEAD_DIM), HEAD_DIM)
        kv_stage[head, i % 2] = v_ref[:, lanes] if i % 2 else rotated(k_ref[:, lanes])
        return carry

    def stage_q(j, peer, carry):
        head = peer * heads_here + j
        lanes = pl.ds(pl.multiple_of(head * HEAD_DIM, HEAD_DIM), HEAD_DIM)
        q_stage[head] = rotated(q_ref[:, lanes])
        return carry

    def send(i):
        if i < 2:
            loads[1 + i].wait()
        lax.fori_loop(0, uly, functools.partial(stage_kv, i), 0)
        if i == 0:
            wait_group()
        exchange(lambda head: kv_stage.at[head, i % 2], kv_in.at[i], kv_ssem.at[i], kv_rsem.at[i], i // 2)

    def queries(j):
        if j == 0:
            loads[3].wait()
        lax.fori_loop(0, uly, functools.partial(stage_q, j), 0)
        exchange(lambda head: q_stage.at[head], q_in.at[j], q_ssem.at[j], q_rsem.at[j], j)

    def exchange(staged, landing, ssem, rsem, j):
        for peer in peers:
            pltpu.make_async_remote_copy(
                src_ref=staged(peer * heads_here + j),
                dst_ref=landing.at[me],
                send_sem=ssem,
                recv_sem=rsem,
                device_id=(blk, peer),
                device_id_type=MESH,
            ).start()
        pltpu.make_async_copy(staged(me * heads_here + j), landing.at[me], rsem).start()

    mine = pl.ds(core * tiles, tiles)
    theirs = pl.ds((1 - core) * tiles, tiles)

    def side(i, slot):
        return wins[i // 2].at[slot, i % 2]

    def to_other(i, slot):
        rows = side(i, slot).at[mine]
        return pltpu.make_async_remote_copy(
            src_ref=rows, dst_ref=rows, send_sem=f_ssem.at[i, slot], recv_sem=f_rsem.at[i, slot],
            device_id=(other, me), device_id_type=MESH,
        )

    def from_other(i, slot):
        rows = side(i, slot).at[theirs]
        return pltpu.make_async_copy(rows, rows, f_rsem.at[i, slot])

    def hop(src, dst, ssem, rsem, target):
        return pltpu.make_async_remote_copy(
            src_ref=src, dst_ref=dst, send_sem=ssem, recv_sem=rsem,
            device_id=(target, me), device_id_type=MESH,
        )

    last = tiles - 1

    def part(n):
        return core * tiles + last if n == 0 else pl.ds(core * tiles, last)

    def to_side(i, slot, target, n):
        return hop(
            side(i, 1).at[part(n)], side(i, 2 - slot).at[part(n)],
            z_ssem.at[i, slot // 2, n], z_rsem.at[i, 1 - slot // 2, n], target,
        )

    def unit(i, slot, n):
        rows = TILE // 2
        return side(i, slot).at[core * tiles + n // 2, pl.ds(n % 2 * rows, rows)]

    def direct(i, slot, target):
        return hop(
            unit(i, 1, DIRECT), unit(i, 2 - slot, DIRECT),
            z_ssem.at[i, slot // 2, 0], z_rsem.at[i, 1 - slot // 2, DIRECT], target,
        )

    def skip_out(i, slot, target):
        return hop(
            unit(i, slot, SKIP), unit(i, 2 - slot, SKIP),
            r_ssem.at[i, 6], z_rsem.at[i, 1 - slot // 2, SKIP], target,
        )

    def bend_in(i, n, which, way, target):
        return hop(
            unit(i, 1, n), relay_buf.at[i, way],
            r_ssem.at[i, which], r_rsem.at[i, way], target,
        )

    def bend_out(i, n, way, target):
        return hop(
            relay_buf.at[i, way], unit(i, 2 * way, n),
            r_ssem.at[i, 4 + way], z_rsem.at[i, way, n], target,
        )

    inner_right = has_right & ~cross_right
    inner_left = has_left & ~cross_left

    def sides(j):
        copies = []
        for which, (n, _, _, shift) in enumerate(bends):
            copies += [
                (cross_right, bend_in(j, n, which, 0, blk - span + shift)),
                (cross_left, bend_in(j, n, which, 1, blk + span - shift)),
            ]
        return copies + [
            (cross_right, direct(j, 2, blk + 2)),
            (cross_left, direct(j, 0, blk - 2)),
            (inner_right, to_side(j, 2, blk + 2, 0)),
            (inner_left, to_side(j, 0, blk - 2, 0)),
            (inner_right, to_side(j, 2, blk + 2, 1)),
            (inner_left, to_side(j, 0, blk - 2, 1)),
        ]

    def relays(j):
        copies = [
            (skip_right, skip_out(j, 2, blk + 4)),
            (skip_left, skip_out(j, 0, blk - 4)),
        ]
        for n, up, down, shift in bends:
            copies += [
                (up, bend_out(j, n, 0, blk + row - shift)),
                (down, bend_out(j, n, 1, blk - row + shift)),
            ]
        return copies

    def start_all(copies):
        for due, copy in copies:

            @pl.when(due)
            def _():
                copy.start()

    def sent_all(copies):
        for due, copy in copies:

            @pl.when(due)
            def _():
                copy.wait_send()

    def arrived(rows, sem):
        pltpu.make_async_copy(rows, rows, sem).wait()

    def gather_rows(landing, index, store):
        for pair in range(uly // 2):
            both = jnp.concatenate(
                [landing[index(2 * pair)].astype(jnp.float32), landing[index(2 * pair + 1)].astype(jnp.float32)],
                axis=0,
            ).astype(jnp.bfloat16)
            first, past = 2 * chunk * pair, 2 * chunk * (pair + 1)
            for tile in range(first // TILE, (past - 1) // TILE + 1):
                start, stop = max(first, tile * TILE), min(past, (tile + 1) * TILE)
                store(tile, start - tile * TILE, both[start - first : stop - first])

    def spread(j):
        arrived(kv_in.at[j], kv_rsem.at[j])

        def store(tile, row, value):
            wins[j // 2][1, j % 2, core * tiles + tile, pl.ds(row, value.shape[0])] = value

        gather_rows(kv_in, lambda s: (j, s), store)
        if j == 0:
            wait_columns()
        start_all(sides(j))
        to_other(j, 1).start()

    def relay(j):
        for _, up, down, _ in bends:
            for way, due in ((0, up), (1, down)):

                @pl.when(due)
                def _():
                    arrived(relay_buf.at[j, way], r_rsem.at[j, way])

        for slot, due in ((0, skip_left), (2, skip_right)):

            @pl.when(due)
            def _():
                arrived(side(j, slot).at[part(0)], z_rsem.at[j, slot // 2, 0])

        start_all(relays(j))

    def forward(j):
        for slot, inner, skips, cross in (
            (0, inner_left, skip_left, cross_left),
            (2, inner_right, skip_right, cross_right),
        ):

            @pl.when(inner)
            def _():
                @pl.when(~skips)
                def _():
                    arrived(side(j, slot).at[part(0)], z_rsem.at[j, slot // 2, 0])

                arrived(side(j, slot).at[part(1)], z_rsem.at[j, slot // 2, 1])
                to_other(j, slot).start()

            @pl.when(cross)
            def _():
                for n in range(2 * tiles):
                    arrived(unit(j, slot, n), z_rsem.at[j, slot // 2, n])
                to_other(j, slot).start()

    factor = HEAD_DIM ** -0.5 * math.log2(math.e)
    listed = KPT // 2

    def attend(j):
        pltpu.make_async_copy(q_in.at[j], q_in.at[j], q_rsem.at[j]).wait()
        def store(tile, row, value):
            q_rows[tile, pl.ds(row, value.shape[0])] = value
        gather_rows(q_in, lambda s: (j, s), store)
        for i in (2 * j, 2 * j + 1):
            from_other(i, 1).wait()

            @pl.when(has_left)
            def _():
                from_other(i, 0).wait()

            @pl.when(has_right)
            def _():
                from_other(i, 2).wait()

        lanes = pl.ds(pl.multiple_of((me * heads_here + j) * HEAD_DIM, HEAD_DIM), HEAD_DIM)
        for tile in range(tiles):
            side, first = choice[tile]

            def rows_of(slot, which):
                return jnp.concatenate(
                    [wins[j][slot, which, first + step] for step in range(listed)], axis=0
                )

            query = q_rows[tile]
            contract = (((1,), (1,)), ((), ()))
            near = lax.dot_general(
                query, rows_of(1, 0), contract, preferred_element_type=jnp.float32
            )
            far = lax.dot_general(
                query, rows_of(side, 0), contract, preferred_element_type=jnp.float32
            )
            largest = jnp.maximum(
                jnp.max(near, axis=1, keepdims=True), jnp.max(far, axis=1, keepdims=True)
            )
            near = jnp.exp2((near - largest) * factor)
            far = jnp.exp2((far - largest) * factor)
            total = jnp.sum(near, axis=1, keepdims=True) + jnp.sum(far, axis=1, keepdims=True)
            summed = jnp.dot(
                near.astype(jnp.bfloat16), rows_of(1, 1), preferred_element_type=jnp.float32
            ) + jnp.dot(
                far.astype(jnp.bfloat16), rows_of(side, 1), preferred_element_type=jnp.float32
            )
            o_rows[pl.ds(tile * TILE, TILE)] = summed / total
            for part_ in range(tile * TILE // chunk, (tile + 1) * TILE // chunk):
                o_stage[j, part_] = o_rows[pl.ds(part_ * chunk, chunk)].astype(jnp.bfloat16)

                @pl.when(me == part_)
                def _():
                    pltpu.make_async_copy(
                        o_stage.at[j, part_], out_ref.at[:, lanes], o_rsem
                    ).start()

                @pl.when(me != part_)
                def _():
                    pltpu.make_async_remote_copy(
                        src_ref=o_stage.at[j, part_],
                        dst_ref=out_ref.at[:, lanes],
                        send_sem=o_ssem.at[j],
                        recv_sem=o_rsem,
                        device_id=(blk, part_),
                        device_id_type=MESH,
                    ).start()

    choice = []

    def choose():
        loads[4].wait()

        for tile in range(tiles):
            here = blk * tiles + tile
            lowest = pairs[0, here]
            for slot in range(1, KPT):
                lowest = jnp.minimum(lowest, pairs[slot, here])
            across = lax.div(lowest, GF * GH)
            choice.append((
                jnp.where(across < col, 0, 2),
                jnp.clip(lowest - across * (GF * GH), 0, GF * GH - KPT // 2),
            ))

    sent = pl.ds(0, uly - 1)

    def left(like, ssem, j):
        pltpu.make_async_copy(like.at[j, sent], like.at[j, sent], ssem.at[j]).wait()

    send(0)
    send(1)
    choose()
    left(kv_in, kv_ssem, 0)
    send(2)
    spread(0)
    left(kv_in, kv_ssem, 1)
    send(3)
    spread(1)
    left(kv_in, kv_ssem, 2)
    send(4)
    relay(0)
    spread(2)
    left(kv_in, kv_ssem, 3)
    send(5)
    relay(1)
    forward(0)
    spread(3)
    left(kv_in, kv_ssem, 4)
    queries(0)
    relay(2)
    forward(1)
    spread(4)
    left(kv_in, kv_ssem, 5)
    queries(1)
    relay(3)
    forward(2)
    spread(5)
    left(q_in, q_ssem, 0)
    queries(2)
    relay(4)
    attend(0)
    forward(3)
    relay(5)
    attend(1)
    forward(4)
    forward(5)
    attend(2)
    for j in range(heads_here):
        if j == 1:
            left(q_in, q_ssem, j)
        if j == 2:
            left(q_in, q_ssem, j)
        left(o_stage, o_ssem, j)
    for i in range(2 * heads_here):
        to_other(i, 1).wait_send()
        sent_all(sides(i) + relays(i))
        sent_all(((has_left, to_other(i, 0)), (has_right, to_other(i, 2))))
    pltpu.make_async_copy(out_ref, out_ref, o_rsem).wait()


def on_device(cols, line, queries, keys, values, tile_pairs, tile_coords):
    uly = lax.axis_size("uly")
    chunk, columns = queries.shape
    heads_here = columns // HEAD_DIM // uly
    run = chunk * uly
    tiles = run // TILE
    vmem = pl.BlockSpec(memory_space=pltpu.VMEM)
    dma = pltpu.SemaphoreType.DMA
    bf16 = jnp.bfloat16
    heads = uly * heads_here
    window = pltpu.VMEM((3, 2, 2 * tiles, TILE, HEAD_DIM), bf16)
    stages = 2 * heads_here
    return pl.pallas_call(
        functools.partial(kernel, uly, heads_here, cols, line),
        out_shape=jax.ShapeDtypeStruct(queries.shape, bf16),
        in_specs=[pl.BlockSpec(memory_space=pltpu.HBM)] * 5,
        out_specs=vmem,
        scratch_shapes=[
            pltpu.VMEM((heads, 2, chunk, HEAD_DIM), bf16),
            pltpu.VMEM((heads, chunk, HEAD_DIM), bf16),
            pltpu.VMEM((stages, uly, chunk, HEAD_DIM), bf16),
            pltpu.VMEM((heads_here, uly, chunk, HEAD_DIM), bf16),
            window, window, window,
            pltpu.VMEM((tiles, TILE, HEAD_DIM), bf16),
            pltpu.VMEM((run, HEAD_DIM), jnp.float32),
            pltpu.VMEM((heads_here, uly, chunk, HEAD_DIM), bf16),
            dma((stages,)), dma((stages,)),
            dma((heads_here,)), dma((heads_here,)),
            dma((stages, 2, 2)), dma((stages, 2, 2 * tiles)),
            dma((stages, 3)), dma((stages, 3)),
            dma((heads_here,)), dma(()),
            pltpu.VMEM((stages, 2, TILE // 2, HEAD_DIM), bf16), dma((stages, 7)), dma((stages, 2)),
            pltpu.VMEM(queries.shape, bf16), pltpu.VMEM(queries.shape, bf16), pltpu.VMEM(queries.shape, bf16),
            pltpu.SMEM(tile_pairs.shape[::-1], jnp.int32), pltpu.SMEM(tile_coords.shape[::-1], jnp.int32), dma((5,)), pltpu.SemaphoreType.REGULAR,
        ],
        compiler_params=pltpu.CompilerParams(
            collective_id=0, has_side_effects=True, vmem_limit_bytes=56 * 2 ** 20
        ),
    )(queries, keys, values, tile_pairs.T, tile_coords.T)


def solution(mesh):
    spec = P(("blk", "uly"), None)
    return jax.shard_map(
        functools.partial(on_device, mesh.shape["blk"] // 2, LINE),
        mesh=mesh,
        in_specs=(spec, spec, spec, P(), P()),
        out_specs=spec,
        check_vma=False,
    )
```

```python
import functools
import math

import jax
import jax.numpy as jnp
from jax import lax
from jax.experimental import pallas as pl
from jax.experimental.pallas import tpu as pltpu
from jax.sharding import PartitionSpec as P

HEAD_DIM = 128
TF = 3
TH = 8
TW = 8
GF = 2
GH = 3
KPT = 8
TILE = 192
LINE = 8
MESH = pl.DeviceIdType.MESH
DIRECT = 0
SKIP = 4
BENDS = ((1, 0), (2, 1), (3, 2), (5, 5))


def rope_tables(coords, row, offset, count):
    shape = (count, HEAD_DIM)
    token = lax.broadcasted_iota(jnp.int32, shape, 0) + offset
    lane = lax.broadcasted_iota(jnp.int32, shape, 1)
    past = token >= TILE
    token = jnp.where(past, token - TILE, token)
    last = row + lax.div(offset + count - 1, TILE)

    def cell(axis):
        return jnp.where(past, coords[axis, last], coords[axis, row])

    halves = HEAD_DIM // 2
    side_pairs = HEAD_DIM // 6
    frame_pairs = halves - 2 * side_pairs
    pair = jnp.where(lane < halves, lane, lane - halves)
    in_frame = pair < frame_pairs
    in_height = pair < frame_pairs + side_pairs
    within = jnp.where(
        in_frame, pair, jnp.where(in_height, pair - frame_pairs, pair - frame_pairs - side_pairs)
    ).astype(jnp.float32)
    axis_len = jnp.where(in_frame, float(frame_pairs), float(side_pairs))
    frequency = jnp.exp(-math.log(10000.0) * within / axis_len)
    position = jnp.where(
        in_frame,
        cell(0) * TF + lax.div(token, TH * TW),
        jnp.where(
            in_height,
            cell(1) * TH + lax.rem(lax.div(token, TW), TH),
            cell(2) * TW + lax.rem(token, TW),
        ),
    ).astype(jnp.float32)
    angles = position * frequency
    return jnp.cos(angles), jnp.where(lane < halves, -jnp.sin(angles), jnp.sin(angles))


def kernel(
    uly, heads_here, cols, line,
    q_hbm, k_hbm, v_hbm, pairs_hbm, coords_hbm,
    out_ref,
    kv_stage, q_stage, kv_in, q_in, win0, win1, win2, q_rows, o_rows, o_stage,
    kv_ssem, kv_rsem, q_ssem, q_rsem, z_ssem, z_rsem, f_ssem, f_rsem, o_ssem, o_rsem,
    relay_buf, r_ssem, r_rsem, q_ref, k_ref, v_ref, pairs, coords, in_sem, go_sem,
):
    wins = (win0, win1, win2)
    heads = uly * heads_here
    chunk = q_ref.shape[0]
    run = chunk * uly
    blk = lax.axis_index("blk")
    me = lax.axis_index("uly")
    tiles = run // TILE
    loads = [
        pltpu.make_async_copy(src, dst, in_sem.at[n])
        for n, (src, dst) in enumerate((
            (coords_hbm, coords),
            (k_hbm, k_ref),
            (v_hbm, v_ref),
            (q_hbm, q_ref),
            (pairs_hbm, pairs),
        ))
    ]
    for load in loads:
        load.start()
    core = lax.rem(blk, 2)
    col = lax.div(blk, 2)
    has_left = col > 0
    has_right = col < cols - 1
    place = lax.rem(col, line)
    cross_left = (place == 0) & has_left
    cross_right = (place == line - 1) & has_right
    skip_right = (place == line - 2) & (col < cols - line)
    skip_left = (place == 1) & (col >= line)
    row = 2 * line
    span = row - 2
    bends = [
        (unit, (place == stop) & (col < cols - line), (place == line - 1 - stop) & (col >= line), 2 * stop)
        for unit, stop in BENDS
    ]
    peers = [lax.rem(me + step, uly) for step in (1, 3, 5, 7, 2, 6, 4)]
    other = blk + 1 - 2 * core

    barrier = pltpu.get_barrier_semaphore()
    for peer in peers:
        pl.semaphore_signal(barrier, inc=1, device_id=(blk - core, peer), device_id_type=MESH)
    pl.semaphore_signal(barrier, inc=1, device_id=(other, me), device_id_type=MESH)
    greeted = [
        (has_left, blk - 2),
        (has_right, blk + 2),
        (cross_left, blk - 4),
        (cross_right, blk + 4),
        (skip_right, blk + 4),
        (skip_left, blk - 4),
    ]
    for _, up, down, shift in bends:
        greeted += [
            (cross_left, blk + span - shift),
            (cross_left, blk - row + shift),
            (cross_right, blk - span + shift),
            (cross_right, blk + row - shift),
            (up, blk + span - shift),
            (up, blk + row - shift),
            (down, blk - span + shift),
            (down, blk - row + shift),
        ]
    columns_in = 0
    for due, target in greeted:
        columns_in = columns_in + due.astype(jnp.int32)

        @pl.when(due)
        def _():
            pl.semaphore_signal(
                barrier, inc=1, device_id=(target - core + 1, me), device_id_type=MESH
            )

    def tell_other():
        pl.semaphore_signal(go_sem, inc=1, device_id=(other, me), device_id_type=MESH)

    def wait_group():
        @pl.when(core == 0)
        def _():
            pl.semaphore_wait(barrier, 2 * (uly - 1) + 1)
            tell_other()

        @pl.when(core == 1)
        def _():
            pl.semaphore_wait(go_sem, 1)

    def wait_columns():
        @pl.when(core == 1)
        def _():
            pl.semaphore_wait(barrier, 2 * columns_in + 1)
            tell_other()

        @pl.when(core == 0)
        def _():
            pl.semaphore_wait(go_sem, 1)

    loads[0].wait()
    cosine, sine = rope_tables(
        coords,
        blk * tiles + lax.div(me * chunk, TILE),
        lax.rem(me * chunk, TILE),
        chunk,
    )

    def rotated(rows):
        rows = rows.astype(jnp.float32)
        return (rows * cosine + pltpu.roll(rows, HEAD_DIM // 2, 1) * sine).astype(jnp.bfloat16)

    def stage_kv(i, peer, carry):
        head = peer * heads_here + i // 2
        lanes = pl.ds(pl.multiple_of(head * HEAD_DIM, HEAD_DIM), HEAD_DIM)
        kv_stage[head, i % 2] = v_ref[:, lanes] if i % 2 else rotated(k_ref[:, lanes])
        return carry

    def stage_q(j, peer, carry):
        head = peer * heads_here + j
        lanes = pl.ds(pl.multiple_of(head * HEAD_DIM, HEAD_DIM), HEAD_DIM)
        q_stage[head] = rotated(q_ref[:, lanes])
        return carry

    def send(i):
        if i < 2:
            loads[1 + i].wait()
        lax.fori_loop(0, uly, functools.partial(stage_kv, i), 0)
        if i == 0:
            wait_group()
        exchange(lambda head: kv_stage.at[head, i % 2], kv_in.at[i], kv_ssem.at[i], kv_rsem.at[i], i // 2)

    def queries(j):
        if j == 0:
            loads[3].wait()
        lax.fori_loop(0, uly, functools.partial(stage_q, j), 0)
        exchange(lambda head: q_stage.at[head], q_in.at[j], q_ssem.at[j], q_rsem.at[j], j)

    def exchange(staged, landing, ssem, rsem, j):
        for peer in peers:
            pltpu.make_async_remote_copy(
                src_ref=staged(peer * heads_here + j),
                dst_ref=landing.at[me],
                send_sem=ssem,
                recv_sem=rsem,
                device_id=(blk, peer),
                device_id_type=MESH,
            ).start()
        pltpu.make_async_copy(staged(me * heads_here + j), landing.at[me], rsem).start()

    mine = pl.ds(core * tiles, tiles)
    theirs = pl.ds((1 - core) * tiles, tiles)

    def side(i, slot):
        return wins[i // 2].at[slot, i % 2]

    def to_other(i, slot):
        rows = side(i, slot).at[mine]
        return pltpu.make_async_remote_copy(
            src_ref=rows, dst_ref=rows, send_sem=f_ssem.at[i, slot], recv_sem=f_rsem.at[i, slot],
            device_id=(other, me), device_id_type=MESH,
        )

    def from_other(i, slot):
        rows = side(i, slot).at[theirs]
        return pltpu.make_async_copy(rows, rows, f_rsem.at[i, slot])

    def hop(src, dst, ssem, rsem, target):
        return pltpu.make_async_remote_copy(
            src_ref=src, dst_ref=dst, send_sem=ssem, recv_sem=rsem,
            device_id=(target, me), device_id_type=MESH,
        )

    last = tiles - 1

    def part(n):
        return core * tiles + last if n == 0 else pl.ds(core * tiles, last)

    def to_side(i, slot, target, n):
        return hop(
            side(i, 1).at[part(n)], side(i, 2 - slot).at[part(n)],
            z_ssem.at[i, slot // 2, n], z_rsem.at[i, 1 - slot // 2, n], target,
        )

    def unit(i, slot, n):
        rows = TILE // 2
        return side(i, slot).at[core * tiles + n // 2, pl.ds(n % 2 * rows, rows)]

    def direct(i, slot, target):
        return hop(
            unit(i, 1, DIRECT), unit(i, 2 - slot, DIRECT),
            z_ssem.at[i, slot // 2, 0], z_rsem.at[i, 1 - slot // 2, DIRECT], target,
        )

    def skip_out(i, slot, target):
        return hop(
            unit(i, slot, SKIP), unit(i, 2 - slot, SKIP),
            r_ssem.at[i, 6], z_rsem.at[i, 1 - slot // 2, SKIP], target,
        )

    def bend_in(i, n, which, way, target):
        return hop(
            unit(i, 1, n), relay_buf.at[i, way],
            r_ssem.at[i, which], r_rsem.at[i, way], target,
        )

    def bend_out(i, n, way, target):
        return hop(
            relay_buf.at[i, way], unit(i, 2 * way, n),
            r_ssem.at[i, 4 + way], z_rsem.at[i, way, n], target,
        )

    inner_right = has_right & ~cross_right
    inner_left = has_left & ~cross_left

    def sides(j):
        copies = []
        for which, (n, _, _, shift) in enumerate(bends):
            copies += [
                (cross_right, bend_in(j, n, which, 0, blk - span + shift)),
                (cross_left, bend_in(j, n, which, 1, blk + span - shift)),
            ]
        return copies + [
            (cross_right, direct(j, 2, blk + 2)),
            (cross_left, direct(j, 0, blk - 2)),
            (inner_right, to_side(j, 2, blk + 2, 0)),
            (inner_left, to_side(j, 0, blk - 2, 0)),
            (inner_right, to_side(j, 2, blk + 2, 1)),
            (inner_left, to_side(j, 0, blk - 2, 1)),
        ]

    def relays(j):
        copies = [
            (skip_right, skip_out(j, 2, blk + 4)),
            (skip_left, skip_out(j, 0, blk - 4)),
        ]
        for n, up, down, shift in bends:
            copies += [
                (up, bend_out(j, n, 0, blk + row - shift)),
                (down, bend_out(j, n, 1, blk - row + shift)),
            ]
        return copies

    def start_all(copies):
        for due, copy in copies:

            @pl.when(due)
            def _():
                copy.start()

    def sent_all(copies):
        for due, copy in copies:

            @pl.when(due)
            def _():
                copy.wait_send()

    def arrived(rows, sem):
        pltpu.make_async_copy(rows, rows, sem).wait()

    def gather_rows(landing, index, store):
        for pair in range(uly // 2):
            both = jnp.concatenate(
                [landing[index(2 * pair)].astype(jnp.float32), landing[index(2 * pair + 1)].astype(jnp.float32)],
                axis=0,
            ).astype(jnp.bfloat16)
            first, past = 2 * chunk * pair, 2 * chunk * (pair + 1)
            for tile in range(first // TILE, (past - 1) // TILE + 1):
                start, stop = max(first, tile * TILE), min(past, (tile + 1) * TILE)
                store(tile, start - tile * TILE, both[start - first : stop - first])

    def spread(j):
        arrived(kv_in.at[j], kv_rsem.at[j])

        def store(tile, row, value):
            wins[j // 2][1, j % 2, core * tiles + tile, pl.ds(row, value.shape[0])] = value

        gather_rows(kv_in, lambda s: (j, s), store)
        if j == 0:
            wait_columns()
        start_all(sides(j))
        to_other(j, 1).start()

    def relay(j):
        for _, up, down, _ in bends:
            for way, due in ((0, up), (1, down)):

                @pl.when(due)
                def _():
                    arrived(relay_buf.at[j, way], r_rsem.at[j, way])

        for slot, due in ((0, skip_left), (2, skip_right)):

            @pl.when(due)
            def _():
                arrived(side(j, slot).at[part(0)], z_rsem.at[j, slot // 2, 0])

        start_all(relays(j))

    def forward(j):
        for slot, inner, skips, cross in (
            (0, inner_left, skip_left, cross_left),
            (2, inner_right, skip_right, cross_right),
        ):

            @pl.when(inner)
            def _():
                @pl.when(~skips)
                def _():
                    arrived(side(j, slot).at[part(0)], z_rsem.at[j, slot // 2, 0])

                arrived(side(j, slot).at[part(1)], z_rsem.at[j, slot // 2, 1])
                to_other(j, slot).start()

            @pl.when(cross)
            def _():
                for n in range(2 * tiles):
                    arrived(unit(j, slot, n), z_rsem.at[j, slot // 2, n])
                to_other(j, slot).start()

    factor = HEAD_DIM ** -0.5 * math.log2(math.e)
    listed = KPT // 2

    def attend(j):
        pltpu.make_async_copy(q_in.at[j], q_in.at[j], q_rsem.at[j]).wait()
        def store(tile, row, value):
            q_rows[tile, pl.ds(row, value.shape[0])] = value
        gather_rows(q_in, lambda s: (j, s), store)
        for i in (2 * j, 2 * j + 1):
            from_other(i, 1).wait()

            @pl.when(has_left)
            def _():
                from_other(i, 0).wait()

            @pl.when(has_right)
            def _():
                from_other(i, 2).wait()

        lanes = pl.ds(pl.multiple_of((me * heads_here + j) * HEAD_DIM, HEAD_DIM), HEAD_DIM)
        for tile in range(tiles):
            side, first = choice[tile]

            def rows_of(slot, which):
                return jnp.concatenate(
                    [wins[j][slot, which, first + step] for step in range(listed)], axis=0
                )

            query = q_rows[tile]
            contract = (((1,), (1,)), ((), ()))
            near = lax.dot_general(
                query, rows_of(1, 0), contract, preferred_element_type=jnp.float32
            )
            far = lax.dot_general(
                query, rows_of(side, 0), contract, preferred_element_type=jnp.float32
            )
            largest = jnp.maximum(
                jnp.max(near, axis=1, keepdims=True), jnp.max(far, axis=1, keepdims=True)
            )
            near = jnp.exp2((near - largest) * factor)
            far = jnp.exp2((far - largest) * factor)
            total = jnp.sum(near, axis=1, keepdims=True) + jnp.sum(far, axis=1, keepdims=True)
            summed = jnp.dot(
                near.astype(jnp.bfloat16), rows_of(1, 1), preferred_element_type=jnp.float32
            ) + jnp.dot(
                far.astype(jnp.bfloat16), rows_of(side, 1), preferred_element_type=jnp.float32
            )
            o_rows[pl.ds(tile * TILE, TILE)] = summed / total
            for part_ in range(tile * TILE // chunk, (tile + 1) * TILE // chunk):
                o_stage[j, part_] = o_rows[pl.ds(part_ * chunk, chunk)].astype(jnp.bfloat16)

                @pl.when(me == part_)
                def _():
                    pltpu.make_async_copy(
                        o_stage.at[j, part_], out_ref.at[:, lanes], o_rsem
                    ).start()

                @pl.when(me != part_)
                def _():
                    pltpu.make_async_remote_copy(
                        src_ref=o_stage.at[j, part_],
                        dst_ref=out_ref.at[:, lanes],
                        send_sem=o_ssem.at[j],
                        recv_sem=o_rsem,
                        device_id=(blk, part_),
                        device_id_type=MESH,
                    ).start()

    choice = []

    def choose():
        loads[4].wait()

        for tile in range(tiles):
            here = blk * tiles + tile
            lowest = pairs[0, here]
            for slot in range(1, KPT):
                lowest = jnp.minimum(lowest, pairs[slot, here])
            across = lax.div(lowest, GF * GH)
            choice.append((
                jnp.where(across < col, 0, 2),
                jnp.clip(lowest - across * (GF * GH), 0, GF * GH - KPT // 2),
            ))

    sent = pl.ds(0, uly - 1)

    def left(like, ssem, j):
        pltpu.make_async_copy(like.at[j, sent], like.at[j, sent], ssem.at[j]).wait()

    send(0)
    send(1)
    choose()
    left(kv_in, kv_ssem, 0)
    send(2)
    spread(0)
    left(kv_in, kv_ssem, 1)
    send(3)
    spread(1)
    left(kv_in, kv_ssem, 2)
    send(4)
    relay(0)
    spread(2)
    left(kv_in, kv_ssem, 3)
    send(5)
    relay(1)
    spread(3)
    left(kv_in, kv_ssem, 4)
    queries(0)
    relay(2)
    forward(0)
    spread(4)
    left(kv_in, kv_ssem, 5)
    queries(1)
    relay(3)
    forward(1)
    spread(5)
    left(q_in, q_ssem, 0)
    queries(2)
    relay(4)
    forward(2)
    forward(3)
    relay(5)
    attend(0)
    forward(4)
    attend(1)
    forward(5)
    attend(2)
    for j in range(heads_here):
        if j == 1:
            left(q_in, q_ssem, j)
        if j == 2:
            left(q_in, q_ssem, j)
        left(o_stage, o_ssem, j)
    for i in range(2 * heads_here):
        to_other(i, 1).wait_send()
        sent_all(sides(i) + relays(i))
        sent_all(((has_left, to_other(i, 0)), (has_right, to_other(i, 2))))
    pltpu.make_async_copy(out_ref, out_ref, o_rsem).wait()


def on_device(cols, line, queries, keys, values, tile_pairs, tile_coords):
    uly = lax.axis_size("uly")
    chunk, columns = queries.shape
    heads_here = columns // HEAD_DIM // uly
    run = chunk * uly
    tiles = run // TILE
    vmem = pl.BlockSpec(memory_space=pltpu.VMEM)
    dma = pltpu.SemaphoreType.DMA
    bf16 = jnp.bfloat16
    heads = uly * heads_here
    window = pltpu.VMEM((3, 2, 2 * tiles, TILE, HEAD_DIM), bf16)
    stages = 2 * heads_here
    return pl.pallas_call(
        functools.partial(kernel, uly, heads_here, cols, line),
        out_shape=jax.ShapeDtypeStruct(queries.shape, bf16),
        in_specs=[pl.BlockSpec(memory_space=pltpu.HBM)] * 5,
        out_specs=pl.BlockSpec(memory_space=pltpu.HBM),
        scratch_shapes=[
            pltpu.VMEM((heads, 2, chunk, HEAD_DIM), bf16),
            pltpu.VMEM((heads, chunk, HEAD_DIM), bf16),
            pltpu.VMEM((stages, uly, chunk, HEAD_DIM), bf16),
            pltpu.VMEM((heads_here, uly, chunk, HEAD_DIM), bf16),
            window, window, window,
            pltpu.VMEM((tiles, TILE, HEAD_DIM), bf16),
            pltpu.VMEM((run, HEAD_DIM), jnp.float32),
            pltpu.VMEM((heads_here, uly, chunk, HEAD_DIM), bf16),
            dma((stages,)), dma((stages,)),
            dma((heads_here,)), dma((heads_here,)),
            dma((stages, 2, 2)), dma((stages, 2, 2 * tiles)),
            dma((stages, 3)), dma((stages, 3)),
            dma((heads_here,)), dma(()),
            pltpu.VMEM((stages, 2, TILE // 2, HEAD_DIM), bf16), dma((stages, 7)), dma((stages, 2)),
            pltpu.VMEM(queries.shape, bf16), pltpu.VMEM(queries.shape, bf16), pltpu.VMEM(queries.shape, bf16),
            pltpu.SMEM(tile_pairs.shape[::-1], jnp.int32), pltpu.SMEM(tile_coords.shape[::-1], jnp.int32), dma((5,)), pltpu.SemaphoreType.REGULAR,
        ],
        compiler_params=pltpu.CompilerParams(
            collective_id=0, has_side_effects=True, vmem_limit_bytes=56 * 2 ** 20
        ),
    )(queries, keys, values, tile_pairs.T, tile_coords.T)


def solution(mesh):
    spec = P(("blk", "uly"), None)
    return jax.shard_map(
        functools.partial(on_device, mesh.shape["blk"] // 2, LINE),
        mesh=mesh,
        in_specs=(spec, spec, spec, P(), P()),
        out_specs=spec,
        check_vma=False,
    )
```

```python
import functools
import math

import jax
import jax.numpy as jnp
from jax import lax
from jax.experimental import pallas as pl
from jax.experimental.pallas import tpu as pltpu
from jax.sharding import PartitionSpec as P

HEAD_DIM = 128
TF = 3
TH = 8
TW = 8
GF = 2
GH = 3
KPT = 8
TILE = 192
LINE = 8
MESH = pl.DeviceIdType.MESH
DIRECT = 0
SKIP = 4
BENDS = ((1, 0), (2, 1), (3, 2), (5, 5))


def rope_tables(coords, row, offset, count):
    shape = (count, HEAD_DIM)
    token = lax.broadcasted_iota(jnp.int32, shape, 0) + offset
    lane = lax.broadcasted_iota(jnp.int32, shape, 1)
    past = token >= TILE
    token = jnp.where(past, token - TILE, token)
    last = row + lax.div(offset + count - 1, TILE)

    def cell(axis):
        return jnp.where(past, coords[axis, last], coords[axis, row])

    halves = HEAD_DIM // 2
    side_pairs = HEAD_DIM // 6
    frame_pairs = halves - 2 * side_pairs
    pair = jnp.where(lane < halves, lane, lane - halves)
    in_frame = pair < frame_pairs
    in_height = pair < frame_pairs + side_pairs
    within = jnp.where(
        in_frame, pair, jnp.where(in_height, pair - frame_pairs, pair - frame_pairs - side_pairs)
    ).astype(jnp.float32)
    axis_len = jnp.where(in_frame, float(frame_pairs), float(side_pairs))
    frequency = jnp.exp(-math.log(10000.0) * within / axis_len)
    position = jnp.where(
        in_frame,
        cell(0) * TF + lax.div(token, TH * TW),
        jnp.where(
            in_height,
            cell(1) * TH + lax.rem(lax.div(token, TW), TH),
            cell(2) * TW + lax.rem(token, TW),
        ),
    ).astype(jnp.float32)
    angles = position * frequency
    return jnp.cos(angles), jnp.where(lane < halves, -jnp.sin(angles), jnp.sin(angles))


def kernel(
    uly, heads_here, cols, line,
    q_hbm, k_hbm, v_hbm, pairs_hbm, coords_hbm,
    out_ref,
    kv_stage, q_stage, kv_in, q_in, win0, win1, win2, q_rows, o_rows, o_stage,
    kv_ssem, kv_rsem, q_ssem, q_rsem, z_ssem, z_rsem, f_ssem, f_rsem, o_ssem, o_rsem,
    relay_buf, r_ssem, r_rsem, q_ref, k_ref, v_ref, pairs, coords, in_sem, go_sem,
):
    wins = (win0, win1, win2)
    heads = uly * heads_here
    chunk = q_ref.shape[0]
    run = chunk * uly
    blk = lax.axis_index("blk")
    me = lax.axis_index("uly")
    tiles = run // TILE
    loads = [
        pltpu.make_async_copy(src, dst, in_sem.at[n])
        for n, (src, dst) in enumerate((
            (coords_hbm, coords),
            (k_hbm, k_ref),
            (v_hbm, v_ref),
            (q_hbm, q_ref),
            (pairs_hbm, pairs),
        ))
    ]
    for load in loads:
        load.start()
    core = lax.rem(blk, 2)
    col = lax.div(blk, 2)
    has_left = col > 0
    has_right = col < cols - 1
    place = lax.rem(col, line)
    cross_left = (place == 0) & has_left
    cross_right = (place == line - 1) & has_right
    skip_right = (place == line - 2) & (col < cols - line)
    skip_left = (place == 1) & (col >= line)
    early = place < 3
    row = 2 * line
    span = row - 2
    bends = [
        (unit, (place == stop) & (col < cols - line), (place == line - 1 - stop) & (col >= line), 2 * stop)
        for unit, stop in BENDS
    ]
    peers = [lax.rem(me + step, uly) for step in (1, 3, 5, 7, 2, 6, 4)]
    other = blk + 1 - 2 * core

    barrier = pltpu.get_barrier_semaphore()
    for peer in peers:
        pl.semaphore_signal(barrier, inc=1, device_id=(blk - core, peer), device_id_type=MESH)
    pl.semaphore_signal(barrier, inc=1, device_id=(other, me), device_id_type=MESH)
    greeted = [
        (has_left, blk - 2),
        (has_right, blk + 2),
        (cross_left, blk - 4),
        (cross_right, blk + 4),
        (skip_right, blk + 4),
        (skip_left, blk - 4),
    ]
    for _, up, down, shift in bends:
        greeted += [
            (cross_left, blk + span - shift),
            (cross_left, blk - row + shift),
            (cross_right, blk - span + shift),
            (cross_right, blk + row - shift),
            (up, blk + span - shift),
            (up, blk + row - shift),
            (down, blk - span + shift),
            (down, blk - row + shift),
        ]
    columns_in = 0
    for due, target in greeted:
        columns_in = columns_in + due.astype(jnp.int32)

        @pl.when(due)
        def _():
            pl.semaphore_signal(
                barrier, inc=1, device_id=(target - core + 1, me), device_id_type=MESH
            )

    def tell_other():
        pl.semaphore_signal(go_sem, inc=1, device_id=(other, me), device_id_type=MESH)

    def wait_group():
        @pl.when(core == 0)
        def _():
            pl.semaphore_wait(barrier, 2 * (uly - 1) + 1)
            tell_other()

        @pl.when(core == 1)
        def _():
            pl.semaphore_wait(go_sem, 1)

    def wait_columns():
        @pl.when(core == 1)
        def _():
            pl.semaphore_wait(barrier, 2 * columns_in + 1)
            tell_other()

        @pl.when(core == 0)
        def _():
            pl.semaphore_wait(go_sem, 1)

    loads[0].wait()
    cosine, sine = rope_tables(
        coords,
        blk * tiles + lax.div(me * chunk, TILE),
        lax.rem(me * chunk, TILE),
        chunk,
    )

    def rotated(rows):
        rows = rows.astype(jnp.float32)
        return (rows * cosine + pltpu.roll(rows, HEAD_DIM // 2, 1) * sine).astype(jnp.bfloat16)

    def stage_kv(i, peer, carry):
        head = peer * heads_here + i // 2
        lanes = pl.ds(pl.multiple_of(head * HEAD_DIM, HEAD_DIM), HEAD_DIM)
        kv_stage[head, i % 2] = v_ref[:, lanes] if i % 2 else rotated(k_ref[:, lanes])
        return carry

    def stage_q(j, peer, carry):
        head = peer * heads_here + j
        lanes = pl.ds(pl.multiple_of(head * HEAD_DIM, HEAD_DIM), HEAD_DIM)
        q_stage[head] = rotated(q_ref[:, lanes])
        return carry

    def send(i):
        if i < 2:
            loads[1 + i].wait()
        lax.fori_loop(0, uly, functools.partial(stage_kv, i), 0)
        if i == 0:
            wait_group()
        exchange(lambda head: kv_stage.at[head, i % 2], kv_in.at[i], kv_ssem.at[i], kv_rsem.at[i], i // 2)

    def queries(j):
        if j == 0:
            loads[3].wait()
        lax.fori_loop(0, uly, functools.partial(stage_q, j), 0)
        exchange(lambda head: q_stage.at[head], q_in.at[j], q_ssem.at[j], q_rsem.at[j], j)

    def exchange(staged, landing, ssem, rsem, j):
        for peer in peers:
            pltpu.make_async_remote_copy(
                src_ref=staged(peer * heads_here + j),
                dst_ref=landing.at[me],
                send_sem=ssem,
                recv_sem=rsem,
                device_id=(blk, peer),
                device_id_type=MESH,
            ).start()
        pltpu.make_async_copy(staged(me * heads_here + j), landing.at[me], rsem).start()

    mine = pl.ds(core * tiles, tiles)
    theirs = pl.ds((1 - core) * tiles, tiles)

    def side(i, slot):
        return wins[i // 2].at[slot, i % 2]

    def to_other(i, slot):
        rows = side(i, slot).at[mine]
        return pltpu.make_async_remote_copy(
            src_ref=rows, dst_ref=rows, send_sem=f_ssem.at[i, slot], recv_sem=f_rsem.at[i, slot],
            device_id=(other, me), device_id_type=MESH,
        )

    def from_other(i, slot):
        rows = side(i, slot).at[theirs]
        return pltpu.make_async_copy(rows, rows, f_rsem.at[i, slot])

    def hop(src, dst, ssem, rsem, target):
        return pltpu.make_async_remote_copy(
            src_ref=src, dst_ref=dst, send_sem=ssem, recv_sem=rsem,
            device_id=(target, me), device_id_type=MESH,
        )

    last = tiles - 1

    def part(n):
        return core * tiles + last if n == 0 else pl.ds(core * tiles, last)

    def to_side(i, slot, target, n):
        return hop(
            side(i, 1).at[part(n)], side(i, 2 - slot).at[part(n)],
            z_ssem.at[i, slot // 2, n], z_rsem.at[i, 1 - slot // 2, n], target,
        )

    def unit(i, slot, n):
        rows = TILE // 2
        return side(i, slot).at[core * tiles + n // 2, pl.ds(n % 2 * rows, rows)]

    def direct(i, slot, target):
        return hop(
            unit(i, 1, DIRECT), unit(i, 2 - slot, DIRECT),
            z_ssem.at[i, slot // 2, 0], z_rsem.at[i, 1 - slot // 2, DIRECT], target,
        )

    def skip_out(i, slot, target):
        return hop(
            unit(i, slot, SKIP), unit(i, 2 - slot, SKIP),
            r_ssem.at[i, 6], z_rsem.at[i, 1 - slot // 2, SKIP], target,
        )

    def bend_in(i, n, which, way, target):
        return hop(
            unit(i, 1, n), relay_buf.at[i, way],
            r_ssem.at[i, which], r_rsem.at[i, way], target,
        )

    def bend_out(i, n, way, target):
        return hop(
            relay_buf.at[i, way], unit(i, 2 * way, n),
            r_ssem.at[i, 4 + way], z_rsem.at[i, way, n], target,
        )

    inner_right = has_right & ~cross_right
    inner_left = has_left & ~cross_left

    def sides(j):
        copies = []
        for which, (n, _, _, shift) in enumerate(bends):
            copies += [
                (cross_right, bend_in(j, n, which, 0, blk - span + shift)),
                (cross_left, bend_in(j, n, which, 1, blk + span - shift)),
            ]
        return copies + [
            (cross_right, direct(j, 2, blk + 2)),
            (cross_left, direct(j, 0, blk - 2)),
            (inner_right, to_side(j, 2, blk + 2, 0)),
            (inner_left, to_side(j, 0, blk - 2, 0)),
            (inner_right, to_side(j, 2, blk + 2, 1)),
            (inner_left, to_side(j, 0, blk - 2, 1)),
        ]

    def relays(j):
        copies = [
            (skip_right, skip_out(j, 2, blk + 4)),
            (skip_left, skip_out(j, 0, blk - 4)),
        ]
        for n, up, down, shift in bends:
            copies += [
                (up, bend_out(j, n, 0, blk + row - shift)),
                (down, bend_out(j, n, 1, blk - row + shift)),
            ]
        return copies

    def start_all(copies):
        for due, copy in copies:

            @pl.when(due)
            def _():
                copy.start()

    def sent_all(copies):
        for due, copy in copies:

            @pl.when(due)
            def _():
                copy.wait_send()

    def arrived(rows, sem):
        pltpu.make_async_copy(rows, rows, sem).wait()

    def gather_rows(landing, index, store):
        for pair in range(uly // 2):
            both = jnp.concatenate(
                [landing[index(2 * pair)].astype(jnp.float32), landing[index(2 * pair + 1)].astype(jnp.float32)],
                axis=0,
            ).astype(jnp.bfloat16)
            first, past = 2 * chunk * pair, 2 * chunk * (pair + 1)
            for tile in range(first // TILE, (past - 1) // TILE + 1):
                start, stop = max(first, tile * TILE), min(past, (tile + 1) * TILE)
                store(tile, start - tile * TILE, both[start - first : stop - first])

    def spread(j):
        arrived(kv_in.at[j], kv_rsem.at[j])

        def store(tile, row, value):
            wins[j // 2][1, j % 2, core * tiles + tile, pl.ds(row, value.shape[0])] = value

        gather_rows(kv_in, lambda s: (j, s), store)
        if j == 0:
            wait_columns()
        start_all(sides(j))
        to_other(j, 1).start()

    def relay(j):
        def pass_on(due, rows, sem, copy):
            @pl.when(due)
            def _():
                arrived(rows, sem)
                copy.start()

        for way, skips, skip in (
            (1, skip_left, skip_out(j, 0, blk - 4)),
            (0, skip_right, skip_out(j, 2, blk + 4)),
        ):
            for n, up, down, shift in bends:
                target = blk - row + shift if way else blk + row - shift
                pass_on(
                    down if way else up, relay_buf.at[j, way], r_rsem.at[j, way],
                    bend_out(j, n, way, target),
                )
            pass_on(skips, side(j, 2 - 2 * way).at[part(0)], z_rsem.at[j, 1 - way, 0], skip)

    def forward(j):
        for slot, inner, skips, cross in (
            (0, inner_left, skip_left, cross_left),
            (2, inner_right, skip_right, cross_right),
        ):

            @pl.when(inner)
            def _():
                @pl.when(~skips)
                def _():
                    arrived(side(j, slot).at[part(0)], z_rsem.at[j, slot // 2, 0])

                arrived(side(j, slot).at[part(1)], z_rsem.at[j, slot // 2, 1])
                to_other(j, slot).start()

            @pl.when(cross)
            def _():
                for n in range(2 * tiles):
                    arrived(unit(j, slot, n), z_rsem.at[j, slot // 2, n])
                to_other(j, slot).start()

    factor = HEAD_DIM ** -0.5 * math.log2(math.e)
    listed = KPT // 2

    def attend(j):
        pltpu.make_async_copy(q_in.at[j], q_in.at[j], q_rsem.at[j]).wait()
        def store(tile, row, value):
            q_rows[tile, pl.ds(row, value.shape[0])] = value
        gather_rows(q_in, lambda s: (j, s), store)
        for i in (2 * j, 2 * j + 1):
            from_other(i, 1).wait()

            @pl.when(has_left)
            def _():
                from_other(i, 0).wait()

            @pl.when(has_right)
            def _():
                from_other(i, 2).wait()

        lanes = pl.ds(pl.multiple_of((me * heads_here + j) * HEAD_DIM, HEAD_DIM), HEAD_DIM)
        for tile in range(tiles):
            side, first = choice[tile]

            def rows_of(slot, which):
                return jnp.concatenate(
                    [wins[j][slot, which, first + step] for step in range(listed)], axis=0
                )

            query = q_rows[tile]
            contract = (((1,), (1,)), ((), ()))
            near = lax.dot_general(
                query, rows_of(1, 0), contract, preferred_element_type=jnp.float32
            )
            far = lax.dot_general(
                query, rows_of(side, 0), contract, preferred_element_type=jnp.float32
            )
            largest = jnp.maximum(
                jnp.max(near, axis=1, keepdims=True), jnp.max(far, axis=1, keepdims=True)
            )
            near = jnp.exp2((near - largest) * factor)
            far = jnp.exp2((far - largest) * factor)
            total = jnp.sum(near, axis=1, keepdims=True) + jnp.sum(far, axis=1, keepdims=True)
            summed = jnp.dot(
                near.astype(jnp.bfloat16), rows_of(1, 1), preferred_element_type=jnp.float32
            ) + jnp.dot(
                far.astype(jnp.bfloat16), rows_of(side, 1), preferred_element_type=jnp.float32
            )
            o_rows[pl.ds(tile * TILE, TILE)] = summed / total
            for part_ in range(tile * TILE // chunk, (tile + 1) * TILE // chunk):
                o_stage[j, part_] = o_rows[pl.ds(part_ * chunk, chunk)].astype(jnp.bfloat16)

                @pl.when(me == part_)
                def _():
                    pltpu.make_async_copy(
                        o_stage.at[j, part_], out_ref.at[:, lanes], o_rsem
                    ).start()

                @pl.when(me != part_)
                def _():
                    pltpu.make_async_remote_copy(
                        src_ref=o_stage.at[j, part_],
                        dst_ref=out_ref.at[:, lanes],
                        send_sem=o_ssem.at[j],
                        recv_sem=o_rsem,
                        device_id=(blk, part_),
                        device_id_type=MESH,
                    ).start()

    choice = []

    def choose():
        loads[4].wait()

        for tile in range(tiles):
            here = blk * tiles + tile
            lowest = pairs[0, here]
            for slot in range(1, KPT):
                lowest = jnp.minimum(lowest, pairs[slot, here])
            across = lax.div(lowest, GF * GH)
            choice.append((
                jnp.where(across < col, 0, 2),
                jnp.clip(lowest - across * (GF * GH), 0, GF * GH - KPT // 2),
            ))

    sent = pl.ds(0, uly - 1)

    def left(like, ssem, j):
        pltpu.make_async_copy(like.at[j, sent], like.at[j, sent], ssem.at[j]).wait()

    send(0)
    send(1)
    choose()
    left(kv_in, kv_ssem, 0)
    send(2)
    spread(0)
    left(kv_in, kv_ssem, 1)
    send(3)
    spread(1)
    left(kv_in, kv_ssem, 2)
    send(4)
    @pl.when(~early)
    def _():
        relay(0)

    spread(2)
    left(kv_in, kv_ssem, 3)
    send(5)
    @pl.when(early)
    def _():
        relay(0)

    relay(1)
    spread(3)
    left(kv_in, kv_ssem, 4)
    queries(0)
    relay(2)
    forward(0)
    spread(4)
    left(kv_in, kv_ssem, 5)
    queries(1)
    relay(3)
    forward(1)
    spread(5)
    left(q_in, q_ssem, 0)
    queries(2)
    relay(4)
    forward(2)
    @pl.when(early)
    def _():
        attend(0)

    forward(3)
    relay(5)
    @pl.when(~early)
    def _():
        attend(0)

    forward(4)
    attend(1)
    forward(5)
    attend(2)
    for j in range(heads_here):
        if j == 1:
            left(q_in, q_ssem, j)
        if j == 2:
            left(q_in, q_ssem, j)
        left(o_stage, o_ssem, j)
    for i in range(2 * heads_here):
        to_other(i, 1).wait_send()
        sent_all(sides(i) + relays(i))
        sent_all(((has_left, to_other(i, 0)), (has_right, to_other(i, 2))))
    pltpu.make_async_copy(out_ref, out_ref, o_rsem).wait()


def on_device(cols, line, queries, keys, values, tile_pairs, tile_coords):
    uly = lax.axis_size("uly")
    chunk, columns = queries.shape
    heads_here = columns // HEAD_DIM // uly
    run = chunk * uly
    tiles = run // TILE
    vmem = pl.BlockSpec(memory_space=pltpu.VMEM)
    dma = pltpu.SemaphoreType.DMA
    bf16 = jnp.bfloat16
    heads = uly * heads_here
    window = pltpu.VMEM((3, 2, 2 * tiles, TILE, HEAD_DIM), bf16)
    stages = 2 * heads_here
    return pl.pallas_call(
        functools.partial(kernel, uly, heads_here, cols, line),
        out_shape=jax.ShapeDtypeStruct(queries.shape, bf16),
        in_specs=[pl.BlockSpec(memory_space=pltpu.HBM)] * 5,
        out_specs=pl.BlockSpec(memory_space=pltpu.HBM),
        scratch_shapes=[
            pltpu.VMEM((heads, 2, chunk, HEAD_DIM), bf16),
            pltpu.VMEM((heads, chunk, HEAD_DIM), bf16),
            pltpu.VMEM((stages, uly, chunk, HEAD_DIM), bf16),
            pltpu.VMEM((heads_here, uly, chunk, HEAD_DIM), bf16),
            window, window, window,
            pltpu.VMEM((tiles, TILE, HEAD_DIM), bf16),
            pltpu.VMEM((run, HEAD_DIM), jnp.float32),
            pltpu.VMEM((heads_here, uly, chunk, HEAD_DIM), bf16),
            dma((stages,)), dma((stages,)),
            dma((heads_here,)), dma((heads_here,)),
            dma((stages, 2, 2)), dma((stages, 2, 2 * tiles)),
            dma((stages, 3)), dma((stages, 3)),
            dma((heads_here,)), dma(()),
            pltpu.VMEM((stages, 2, TILE // 2, HEAD_DIM), bf16), dma((stages, 7)), dma((stages, 2)),
            pltpu.VMEM(queries.shape, bf16), pltpu.VMEM(queries.shape, bf16), pltpu.VMEM(queries.shape, bf16),
            pltpu.SMEM(tile_pairs.shape[::-1], jnp.int32), pltpu.SMEM(tile_coords.shape[::-1], jnp.int32), dma((5,)), pltpu.SemaphoreType.REGULAR,
        ],
        compiler_params=pltpu.CompilerParams(
            collective_id=0, has_side_effects=True, vmem_limit_bytes=56 * 2 ** 20
        ),
    )(queries, keys, values, tile_pairs.T, tile_coords.T)


def solution(mesh):
    spec = P(("blk", "uly"), None)
    return jax.shard_map(
        functools.partial(on_device, mesh.shape["blk"] // 2, LINE),
        mesh=mesh,
        in_specs=(spec, spec, spec, P(), P()),
        out_specs=spec,
        check_vma=False,
    )
```

```python
import functools
import math

import jax
import jax.numpy as jnp
from jax import lax
from jax.experimental import pallas as pl
from jax.experimental.pallas import tpu as pltpu
from jax.sharding import PartitionSpec as P

HEAD_DIM = 128
TF = 3
TH = 8
TW = 8
GF = 2
GH = 3
KPT = 8
TILE = 192
LINE = 8
MESH = pl.DeviceIdType.MESH
DIRECT = 0
SKIP = 4
BENDS = ((1, 0), (2, 1), (3, 2), (5, 5))


def rope_tables(coords, row, offset, count):
    shape = (count, HEAD_DIM)
    token = lax.broadcasted_iota(jnp.int32, shape, 0) + offset
    lane = lax.broadcasted_iota(jnp.int32, shape, 1)
    past = token >= TILE
    token = jnp.where(past, token - TILE, token)
    last = row + lax.div(offset + count - 1, TILE)

    def cell(axis):
        return jnp.where(past, coords[axis, last], coords[axis, row])

    halves = HEAD_DIM // 2
    side_pairs = HEAD_DIM // 6
    frame_pairs = halves - 2 * side_pairs
    pair = jnp.where(lane < halves, lane, lane - halves)
    in_frame = pair < frame_pairs
    in_height = pair < frame_pairs + side_pairs
    within = jnp.where(
        in_frame, pair, jnp.where(in_height, pair - frame_pairs, pair - frame_pairs - side_pairs)
    ).astype(jnp.float32)
    axis_len = jnp.where(in_frame, float(frame_pairs), float(side_pairs))
    frequency = jnp.exp(-math.log(10000.0) * within / axis_len)
    position = jnp.where(
        in_frame,
        cell(0) * TF + lax.div(token, TH * TW),
        jnp.where(
            in_height,
            cell(1) * TH + lax.rem(lax.div(token, TW), TH),
            cell(2) * TW + lax.rem(token, TW),
        ),
    ).astype(jnp.float32)
    angles = position * frequency
    return jnp.cos(angles), jnp.where(lane < halves, -jnp.sin(angles), jnp.sin(angles))


def kernel(
    uly, heads_here, cols, line,
    q_hbm, k_hbm, v_hbm, pairs_hbm, coords_hbm,
    out_ref,
    kv_stage, q_stage, kv_in, q_in, win0, win1, win2, q_rows, o_rows, o_stage,
    kv_ssem, kv_rsem, q_ssem, q_rsem, z_ssem, z_rsem, f_ssem, f_rsem, o_ssem, o_rsem,
    relay_buf, r_ssem, r_rsem, q_ref, k_ref, v_ref, pairs, coords, in_sem, go_sem,
):
    wins = (win0, win1, win2)
    heads = uly * heads_here
    chunk = q_ref.shape[0]
    run = chunk * uly
    blk = lax.axis_index("blk")
    me = lax.axis_index("uly")
    tiles = run // TILE
    loads = [
        pltpu.make_async_copy(src, dst, in_sem.at[n])
        for n, (src, dst) in enumerate((
            (coords_hbm, coords),
            (k_hbm, k_ref),
            (v_hbm, v_ref),
            (q_hbm, q_ref),
            (pairs_hbm, pairs),
        ))
    ]
    for load in loads:
        load.start()
    core = lax.rem(blk, 2)
    col = lax.div(blk, 2)
    has_left = col > 0
    has_right = col < cols - 1
    place = lax.rem(col, line)
    cross_left = (place == 0) & has_left
    cross_right = (place == line - 1) & has_right
    skip_right = (place == line - 2) & (col < cols - line)
    skip_left = (place == 1) & (col >= line)
    early = place < 3
    row = 2 * line
    span = row - 2
    bends = [
        (unit, (place == stop) & (col < cols - line), (place == line - 1 - stop) & (col >= line), 2 * stop)
        for unit, stop in BENDS
    ]
    peers = [lax.rem(me + step, uly) for step in (1, 3, 5, 7, 2, 6, 4)]
    other = blk + 1 - 2 * core

    barrier = pltpu.get_barrier_semaphore()
    for peer in peers:
        pl.semaphore_signal(barrier, inc=1, device_id=(blk - core, peer), device_id_type=MESH)
    pl.semaphore_signal(barrier, inc=1, device_id=(other, me), device_id_type=MESH)
    greeted = [
        (has_left, blk - 2),
        (has_right, blk + 2),
        (cross_left, blk - 4),
        (cross_right, blk + 4),
        (skip_right, blk + 4),
        (skip_left, blk - 4),
    ]
    for _, up, down, shift in bends:
        greeted += [
            (cross_left, blk + span - shift),
            (cross_left, blk - row + shift),
            (cross_right, blk - span + shift),
            (cross_right, blk + row - shift),
            (up, blk + span - shift),
            (up, blk + row - shift),
            (down, blk - span + shift),
            (down, blk - row + shift),
        ]
    columns_in = 0
    for due, target in greeted:
        columns_in = columns_in + due.astype(jnp.int32)

        @pl.when(due)
        def _():
            pl.semaphore_signal(
                barrier, inc=1, device_id=(target - core + 1, me), device_id_type=MESH
            )

    def tell_other():
        pl.semaphore_signal(go_sem, inc=1, device_id=(other, me), device_id_type=MESH)

    def wait_group():
        @pl.when(core == 0)
        def _():
            pl.semaphore_wait(barrier, 2 * (uly - 1) + 1)
            tell_other()

        @pl.when(core == 1)
        def _():
            pl.semaphore_wait(go_sem, 1)

    def wait_columns():
        @pl.when(core == 1)
        def _():
            pl.semaphore_wait(barrier, 2 * columns_in + 1)
            tell_other()

        @pl.when(core == 0)
        def _():
            pl.semaphore_wait(go_sem, 1)

    loads[0].wait()
    cosine, sine = rope_tables(
        coords,
        blk * tiles + lax.div(me * chunk, TILE),
        lax.rem(me * chunk, TILE),
        chunk,
    )

    def rotated(rows):
        rows = rows.astype(jnp.float32)
        return (rows * cosine + pltpu.roll(rows, HEAD_DIM // 2, 1) * sine).astype(jnp.bfloat16)

    def stage_kv(i, peer, carry):
        head = peer * heads_here + i // 2
        lanes = pl.ds(pl.multiple_of(head * HEAD_DIM, HEAD_DIM), HEAD_DIM)
        kv_stage[head, i % 2] = v_ref[:, lanes] if i % 2 else rotated(k_ref[:, lanes])
        return carry

    def stage_q(j, peer, carry):
        head = peer * heads_here + j
        lanes = pl.ds(pl.multiple_of(head * HEAD_DIM, HEAD_DIM), HEAD_DIM)
        q_stage[head] = rotated(q_ref[:, lanes])
        return carry

    def send(i):
        if i < 2:
            loads[1 + i].wait()
            lax.fori_loop(0, uly, functools.partial(stage_kv, i), 0)
        if i == 0:
            wait_group()
        exchange(lambda head: kv_stage.at[head, i % 2], kv_in.at[i], kv_ssem.at[i], kv_rsem.at[i], i // 2)

    def stage_rest():
        for i in range(2, 2 * heads_here):
            lax.fori_loop(0, uly, functools.partial(stage_kv, i), 0)
        loads[3].wait()
        for j in range(heads_here):
            lax.fori_loop(0, uly, functools.partial(stage_q, j), 0)

    def queries(j):
        exchange(lambda head: q_stage.at[head], q_in.at[j], q_ssem.at[j], q_rsem.at[j], j)

    def exchange(staged, landing, ssem, rsem, j):
        for peer in peers:
            pltpu.make_async_remote_copy(
                src_ref=staged(peer * heads_here + j),
                dst_ref=landing.at[me],
                send_sem=ssem,
                recv_sem=rsem,
                device_id=(blk, peer),
                device_id_type=MESH,
            ).start()
        pltpu.make_async_copy(staged(me * heads_here + j), landing.at[me], rsem).start()

    mine = pl.ds(core * tiles, tiles)
    theirs = pl.ds((1 - core) * tiles, tiles)

    def side(i, slot):
        return wins[i // 2].at[slot, i % 2]

    def to_other(i, slot):
        rows = side(i, slot).at[mine]
        return pltpu.make_async_remote_copy(
            src_ref=rows, dst_ref=rows, send_sem=f_ssem.at[i, slot], recv_sem=f_rsem.at[i, slot],
            device_id=(other, me), device_id_type=MESH,
        )

    def from_other(i, slot):
        rows = side(i, slot).at[theirs]
        return pltpu.make_async_copy(rows, rows, f_rsem.at[i, slot])

    def hop(src, dst, ssem, rsem, target):
        return pltpu.make_async_remote_copy(
            src_ref=src, dst_ref=dst, send_sem=ssem, recv_sem=rsem,
            device_id=(target, me), device_id_type=MESH,
        )

    last = tiles - 1

    def part(n):
        return core * tiles + last if n == 0 else pl.ds(core * tiles, last)

    def to_side(i, slot, target, n):
        return hop(
            side(i, 1).at[part(n)], side(i, 2 - slot).at[part(n)],
            z_ssem.at[i, slot // 2, n], z_rsem.at[i, 1 - slot // 2, n], target,
        )

    def unit(i, slot, n):
        rows = TILE // 2
        return side(i, slot).at[core * tiles + n // 2, pl.ds(n % 2 * rows, rows)]

    def direct(i, slot, target):
        return hop(
            unit(i, 1, DIRECT), unit(i, 2 - slot, DIRECT),
            z_ssem.at[i, slot // 2, 0], z_rsem.at[i, 1 - slot // 2, DIRECT], target,
        )

    def skip_out(i, slot, target):
        return hop(
            unit(i, slot, SKIP), unit(i, 2 - slot, SKIP),
            r_ssem.at[i, 6], z_rsem.at[i, 1 - slot // 2, SKIP], target,
        )

    def bend_in(i, n, which, way, target):
        return hop(
            unit(i, 1, n), relay_buf.at[i, way],
            r_ssem.at[i, which], r_rsem.at[i, way], target,
        )

    def bend_out(i, n, way, target):
        return hop(
            relay_buf.at[i, way], unit(i, 2 * way, n),
            r_ssem.at[i, 4 + way], z_rsem.at[i, way, n], target,
        )

    inner_right = has_right & ~cross_right
    inner_left = has_left & ~cross_left

    def sides(j):
        copies = []
        for which, (n, _, _, shift) in enumerate(bends):
            copies += [
                (cross_right, bend_in(j, n, which, 0, blk - span + shift)),
                (cross_left, bend_in(j, n, which, 1, blk + span - shift)),
            ]
        return copies + [
            (cross_right, direct(j, 2, blk + 2)),
            (cross_left, direct(j, 0, blk - 2)),
            (inner_right, to_side(j, 2, blk + 2, 0)),
            (inner_left, to_side(j, 0, blk - 2, 0)),
            (inner_right, to_side(j, 2, blk + 2, 1)),
            (inner_left, to_side(j, 0, blk - 2, 1)),
        ]

    def relays(j):
        copies = [
            (skip_right, skip_out(j, 2, blk + 4)),
            (skip_left, skip_out(j, 0, blk - 4)),
        ]
        for n, up, down, shift in bends:
            copies += [
                (up, bend_out(j, n, 0, blk + row - shift)),
                (down, bend_out(j, n, 1, blk - row + shift)),
            ]
        return copies

    def start_all(copies):
        for due, copy in copies:

            @pl.when(due)
            def _():
                copy.start()

    def sent_all(copies):
        for due, copy in copies:

            @pl.when(due)
            def _():
                copy.wait_send()

    def arrived(rows, sem):
        pltpu.make_async_copy(rows, rows, sem).wait()

    def gather_rows(landing, index, store):
        for pair in range(uly // 2):
            both = jnp.concatenate(
                [landing[index(2 * pair)].astype(jnp.float32), landing[index(2 * pair + 1)].astype(jnp.float32)],
                axis=0,
            ).astype(jnp.bfloat16)
            first, past = 2 * chunk * pair, 2 * chunk * (pair + 1)
            for tile in range(first // TILE, (past - 1) // TILE + 1):
                start, stop = max(first, tile * TILE), min(past, (tile + 1) * TILE)
                store(tile, start - tile * TILE, both[start - first : stop - first])

    def spread(j):
        arrived(kv_in.at[j], kv_rsem.at[j])

        def store(tile, row, value):
            wins[j // 2][1, j % 2, core * tiles + tile, pl.ds(row, value.shape[0])] = value

        gather_rows(kv_in, lambda s: (j, s), store)
        if j == 0:
            wait_columns()
        start_all(sides(j))
        to_other(j, 1).start()

    def relay(j):
        def pass_on(due, rows, sem, copy):
            @pl.when(due)
            def _():
                arrived(rows, sem)
                copy.start()

        for way, skips, skip in (
            (1, skip_left, skip_out(j, 0, blk - 4)),
            (0, skip_right, skip_out(j, 2, blk + 4)),
        ):
            for n, up, down, shift in bends:
                target = blk - row + shift if way else blk + row - shift
                pass_on(
                    down if way else up, relay_buf.at[j, way], r_rsem.at[j, way],
                    bend_out(j, n, way, target),
                )
            pass_on(skips, side(j, 2 - 2 * way).at[part(0)], z_rsem.at[j, 1 - way, 0], skip)

    def forward(j):
        for slot, inner, skips, cross in (
            (0, inner_left, skip_left, cross_left),
            (2, inner_right, skip_right, cross_right),
        ):

            @pl.when(inner)
            def _():
                @pl.when(~skips)
                def _():
                    arrived(side(j, slot).at[part(0)], z_rsem.at[j, slot // 2, 0])

                arrived(side(j, slot).at[part(1)], z_rsem.at[j, slot // 2, 1])
                to_other(j, slot).start()

            @pl.when(cross)
            def _():
                for n in range(2 * tiles):
                    arrived(unit(j, slot, n), z_rsem.at[j, slot // 2, n])
                to_other(j, slot).start()

    factor = HEAD_DIM ** -0.5 * math.log2(math.e)
    listed = KPT // 2

    def attend(j):
        pltpu.make_async_copy(q_in.at[j], q_in.at[j], q_rsem.at[j]).wait()
        def store(tile, row, value):
            q_rows[tile, pl.ds(row, value.shape[0])] = value
        gather_rows(q_in, lambda s: (j, s), store)
        for i in (2 * j, 2 * j + 1):
            from_other(i, 1).wait()

            @pl.when(has_left)
            def _():
                from_other(i, 0).wait()

            @pl.when(has_right)
            def _():
                from_other(i, 2).wait()

        lanes = pl.ds(pl.multiple_of((me * heads_here + j) * HEAD_DIM, HEAD_DIM), HEAD_DIM)
        for tile in range(tiles):
            side, first = choice[tile]

            def rows_of(slot, which):
                return jnp.concatenate(
                    [wins[j][slot, which, first + step] for step in range(listed)], axis=0
                )

            query = q_rows[tile]
            contract = (((1,), (1,)), ((), ()))
            near = lax.dot_general(
                query, rows_of(1, 0), contract, preferred_element_type=jnp.float32
            )
            far = lax.dot_general(
                query, rows_of(side, 0), contract, preferred_element_type=jnp.float32
            )
            largest = jnp.maximum(
                jnp.max(near, axis=1, keepdims=True), jnp.max(far, axis=1, keepdims=True)
            )
            near = jnp.exp2((near - largest) * factor)
            far = jnp.exp2((far - largest) * factor)
            total = jnp.sum(near, axis=1, keepdims=True) + jnp.sum(far, axis=1, keepdims=True)
            summed = jnp.dot(
                near.astype(jnp.bfloat16), rows_of(1, 1), preferred_element_type=jnp.float32
            ) + jnp.dot(
                far.astype(jnp.bfloat16), rows_of(side, 1), preferred_element_type=jnp.float32
            )
            o_rows[pl.ds(tile * TILE, TILE)] = summed / total
            for part_ in range(tile * TILE // chunk, (tile + 1) * TILE // chunk):
                o_stage[j, part_] = o_rows[pl.ds(part_ * chunk, chunk)].astype(jnp.bfloat16)

                @pl.when(me == part_)
                def _():
                    pltpu.make_async_copy(
                        o_stage.at[j, part_], out_ref.at[:, lanes], o_rsem
                    ).start()

                @pl.when(me != part_)
                def _():
                    pltpu.make_async_remote_copy(
                        src_ref=o_stage.at[j, part_],
                        dst_ref=out_ref.at[:, lanes],
                        send_sem=o_ssem.at[j],
                        recv_sem=o_rsem,
                        device_id=(blk, part_),
                        device_id_type=MESH,
                    ).start()

    choice = []

    def choose():
        loads[4].wait()

        for tile in range(tiles):
            here = blk * tiles + tile
            lowest = pairs[0, here]
            for slot in range(1, KPT):
                lowest = jnp.minimum(lowest, pairs[slot, here])
            across = lax.div(lowest, GF * GH)
            choice.append((
                jnp.where(across < col, 0, 2),
                jnp.clip(lowest - across * (GF * GH), 0, GF * GH - KPT // 2),
            ))

    sent = pl.ds(0, uly - 1)

    def left(like, ssem, j):
        pltpu.make_async_copy(like.at[j, sent], like.at[j, sent], ssem.at[j]).wait()

    send(0)
    send(1)
    stage_rest()
    choose()
    left(kv_in, kv_ssem, 0)
    send(2)
    spread(0)
    left(kv_in, kv_ssem, 1)
    send(3)
    spread(1)
    left(kv_in, kv_ssem, 2)
    send(4)
    @pl.when(~early)
    def _():
        relay(0)

    spread(2)
    left(kv_in, kv_ssem, 3)
    send(5)
    @pl.when(early)
    def _():
        relay(0)

    relay(1)
    spread(3)
    left(kv_in, kv_ssem, 4)
    queries(0)
    relay(2)
    forward(0)
    spread(4)
    left(kv_in, kv_ssem, 5)
    queries(1)
    relay(3)
    forward(1)
    spread(5)
    left(q_in, q_ssem, 0)
    queries(2)
    relay(4)
    forward(2)
    @pl.when(early)
    def _():
        attend(0)

    forward(3)
    relay(5)
    @pl.when(~early)
    def _():
        attend(0)

    forward(4)
    attend(1)
    forward(5)
    attend(2)
    for j in range(heads_here):
        if j == 1:
            left(q_in, q_ssem, j)
        if j == 2:
            left(q_in, q_ssem, j)
        left(o_stage, o_ssem, j)
    for i in range(2 * heads_here):
        to_other(i, 1).wait_send()
        sent_all(sides(i) + relays(i))
        sent_all(((has_left, to_other(i, 0)), (has_right, to_other(i, 2))))
    pltpu.make_async_copy(out_ref, out_ref, o_rsem).wait()


def on_device(cols, line, queries, keys, values, tile_pairs, tile_coords):
    uly = lax.axis_size("uly")
    chunk, columns = queries.shape
    heads_here = columns // HEAD_DIM // uly
    run = chunk * uly
    tiles = run // TILE
    vmem = pl.BlockSpec(memory_space=pltpu.VMEM)
    dma = pltpu.SemaphoreType.DMA
    bf16 = jnp.bfloat16
    heads = uly * heads_here
    window = pltpu.VMEM((3, 2, 2 * tiles, TILE, HEAD_DIM), bf16)
    stages = 2 * heads_here
    return pl.pallas_call(
        functools.partial(kernel, uly, heads_here, cols, line),
        out_shape=jax.ShapeDtypeStruct(queries.shape, bf16),
        in_specs=[pl.BlockSpec(memory_space=pltpu.HBM)] * 5,
        out_specs=pl.BlockSpec(memory_space=pltpu.HBM),
        scratch_shapes=[
            pltpu.VMEM((heads, 2, chunk, HEAD_DIM), bf16),
            pltpu.VMEM((heads, chunk, HEAD_DIM), bf16),
            pltpu.VMEM((stages, uly, chunk, HEAD_DIM), bf16),
            pltpu.VMEM((heads_here, uly, chunk, HEAD_DIM), bf16),
            window, window, window,
            pltpu.VMEM((tiles, TILE, HEAD_DIM), bf16),
            pltpu.VMEM((run, HEAD_DIM), jnp.float32),
            pltpu.VMEM((heads_here, uly, chunk, HEAD_DIM), bf16),
            dma((stages,)), dma((stages,)),
            dma((heads_here,)), dma((heads_here,)),
            dma((stages, 2, 2)), dma((stages, 2, 2 * tiles)),
            dma((stages, 3)), dma((stages, 3)),
            dma((heads_here,)), dma(()),
            pltpu.VMEM((stages, 2, TILE // 2, HEAD_DIM), bf16), dma((stages, 7)), dma((stages, 2)),
            pltpu.VMEM(queries.shape, bf16), pltpu.VMEM(queries.shape, bf16), pltpu.VMEM(queries.shape, bf16),
            pltpu.SMEM(tile_pairs.shape[::-1], jnp.int32), pltpu.SMEM(tile_coords.shape[::-1], jnp.int32), dma((5,)), pltpu.SemaphoreType.REGULAR,
        ],
        compiler_params=pltpu.CompilerParams(
            collective_id=0, has_side_effects=True, vmem_limit_bytes=56 * 2 ** 20
        ),
    )(queries, keys, values, tile_pairs.T, tile_coords.T)


def solution(mesh):
    spec = P(("blk", "uly"), None)
    return jax.shard_map(
        functools.partial(on_device, mesh.shape["blk"] // 2, LINE),
        mesh=mesh,
        in_specs=(spec, spec, spec, P(), P()),
        out_specs=spec,
        check_vma=False,
    )
```
